32 devices in a mesh: pair: 4 (over z), intg: 8 (over y, x, core).
Axes of the slice: x: 2, y: 2, z: 4, core: 2. Of those that a mesh axis runs over, the one named last changes fastest.
Arguments:
- amplitudes: bfloat16 [1536, 8192], P('pair', 'intg'), may hold values from -6 to 6
- integrals: bfloat16 [4096, 8192], P('pair', 'intg'), may hold values from -0.125 to 0.125
- sym_rows: int32 [32], P('pair'), may hold values from 0 to 3
- sym_cols: int32 [64], P('intg'), may hold values from 0 to 3
- mirror_rows: int32 [4096], replicated, may hold values from 0 to 4095, as said below
Outputs:
- residual: bfloat16 [1536, 4096], P('intg', 'pair')
The draws below stay inside these ranges and needn't reach their ends.
Inputs may be any that keep to these rules, and one draw needn't show every extreme that they name: `mirror_rows`: an involution without fixed points; it maps the rows of each 128-row tile onto all rows of one other tile.
All inputs are finite; a program needn't handle non-finite values.
Results may differ from the reference program's by a relative error of at most 0.001.
Values may be sent and summed in bfloat16 or wider, within the bound.
A program may use at most 128 MiB of HBM per device.

```python
import math
import jax
import jax.numpy as jnp
from jax import lax

TILE = 128
NSYM = 4
IJ = 1536
AB = 4096
CD = 8192


def draw_mirror_rows(key, part):
    key_tiles = jax.random.fold_in(key, 11)
    key_rows = jax.random.fold_in(key, 23)
    count = AB // TILE
    order = jax.random.permutation(key_tiles, count).astype(jnp.int32)
    position = jnp.argsort(order, stable=True).astype(jnp.int32)
    partner = order[position ^ 1]
    leading = position % 2 == 0
    shuffle = jax.random.permutation(key_rows, TILE).astype(jnp.int32)
    inverse = jnp.argsort(shuffle, stable=True).astype(jnp.int32)
    inner = jnp.where(leading[:, None], shuffle[None, :], inverse[None, :])
    mapped = partner[:, None] * TILE + inner
    return mapped.reshape(AB).astype(jnp.int32)


def with_ends(result, rng, least, high):
    longest = result.shape.index(max(result.shape))
    spots = []
    for shift in (0, 1):
        where = [jax.random.randint(jax.random.fold_in(rng, axis), (), 0, length) for axis, length in enumerate(result.shape)]
        where[longest] = (where[longest] + shift) % result.shape[longest]
        spots.append(tuple(where))
    return result.at[spots[0]].set(least).at[spots[1]].set(high)


def block_levels(rng, shape, shards, least, top_value):
    def one(axis_at, parts):
        steps = jax.random.uniform(jax.random.fold_in(jax.random.fold_in(rng, 6), axis_at), (parts,), jnp.float32, least / len(shards), top_value / len(shards))
        return jnp.repeat(jnp.exp(steps), shape[axis_at] // parts).reshape((-1,) + (1,) * (len(shape) - axis_at - 1))

    gain = one(*shards[0])
    for cut in shards[1:]:
        gain = gain * one(*cut)
    return gain


def gaussian(rng, extent, spread, bound, pieces=(), kind=jnp.bfloat16):
    result = spread * jax.random.normal(rng, extent, jnp.float32)
    if pieces:
        result = result * block_levels(rng, extent, pieces, -0.22, 0.18)
    return jnp.clip(result, -bound, bound).astype(kind)


def setup_inputs(seed: int = 0) -> dict:
    seeds = jax.random.split(jax.random.key(seed), 6)
    return {
        "amplitudes": gaussian(seeds[0], (IJ, CD), 1.0, 6.0, ((0, 4), (1, 8))),
        "integrals": gaussian(seeds[1], (AB, CD), (CD // NSYM) ** -0.5, 0.125, ((0, 4), (1, 8))),
        "sym_rows": with_ends(jax.random.randint(seeds[2], (AB // TILE,), 0, NSYM), jax.random.fold_in(seeds[2], 1), 0, NSYM - 1).astype(jnp.int32),
        "sym_cols": with_ends(jax.random.randint(seeds[3], (CD // TILE,), 0, NSYM), jax.random.fold_in(seeds[3], 1), 0, NSYM - 1).astype(jnp.int32),
        "mirror_rows": draw_mirror_rows(jax.random.fold_in(seeds[5], 71), 0),
    }


def reference(amplitudes, integrals, sym_rows, sym_cols, mirror_rows):
    col_block = math.gcd(CD, 4096)
    row_sym = jnp.repeat(sym_rows, TILE)
    col_sym = jnp.repeat(sym_cols, TILE)

    def add_block(index, total):
        start = (index * col_block).astype(jnp.int32)
        values = lax.dynamic_slice_in_dim(integrals, start, col_block, 1)
        labels = lax.dynamic_slice_in_dim(col_sym, start, col_block, 0)
        allowed = jnp.where(row_sym[:, None] == labels[None, :], values, jnp.zeros((), jnp.bfloat16))
        left = lax.dynamic_slice_in_dim(amplitudes, start, col_block, 1)
        return total + lax.dot_general(left, allowed, (((1,), (1,)), ((), ())), preferred_element_type=jnp.float32)

    ladder = lax.fori_loop(0, CD // col_block, add_block, jnp.zeros((IJ, AB), jnp.float32))
    mirrored = jnp.take(ladder, mirror_rows, axis=1)
    return (ladder - mirrored).astype(jnp.bfloat16)
```

```python
import functools

import jax
import jax.numpy as jnp
from jax import lax
from jax.experimental import pallas as pl
from jax.experimental.pallas import tpu as pltpu
from jax.sharding import PartitionSpec as P

MESH = pl.DeviceIdType.MESH
PARTS = 2
CORES = 2
SIDE = 2


def contract_pair(left, right):
    return lax.dot_general(
        left, right, (((1,), (1,)), ((), ())), preferred_element_type=jnp.float32
    )


def shards_plain(amplitudes, integrals, sym_rows, sym_cols, mirror_rows):
    tile_rows = integrals.shape[0] // sym_rows.shape[0]
    row_sym = jnp.repeat(sym_rows, tile_rows)
    col_sym = jnp.repeat(sym_cols, tile_rows)
    masked = jnp.where(row_sym[:, None] == col_sym[None, :], integrals, jnp.zeros((), jnp.bfloat16))
    ab_rows = integrals.shape[0]
    own_twins = lax.dynamic_slice_in_dim(mirror_rows, lax.axis_index("pair") * ab_rows, ab_rows, 0)
    partial_sums = contract_pair(lax.all_gather(amplitudes, "pair", axis=0, tiled=True), masked)
    result_block = lax.psum_scatter(partial_sums, "intg", scatter_dimension=0, tiled=True)
    all_columns = lax.all_gather(result_block, "pair", axis=1, tiled=True)
    result_block = result_block - jnp.take(all_columns, own_twins, axis=1)
    return result_block.astype(jnp.bfloat16)


def ladder_kernel(
    planes, tiles, tile,
    t_ref, v_ref, mask_ref, turn_ref, pick_ref, out_ref,
    v_in, turned, tall, prod, from_core, hop_one, hop_two, cont, from_left, from_right, slots,
    v_sem, t_recv, t_right, t_left, core_send, core_recv,
    a_send, a_recv, b_send, b_recv, a2_send, a2_recv, b2_send, b2_recv,
    zr_send, zr_recv, zl_send, zl_recv, gr_send, gl_send, g_recv,
):
    parts, rows, depth = t_ref.shape[1], t_ref.shape[2], t_ref.shape[3]
    columns = prod.shape[-1]
    half = columns // 2
    group = cont.shape[-1]
    per_plane = group // tile
    last = planes - 1
    p = lax.axis_index("pair")
    g = lax.axis_index("intg")
    core, x, y = g % 2, (g // 2) % 2, g // 4
    chip = g // 2
    sibling = g + 1 - 2 * core
    x_peer = g + 2 - 4 * x
    y_peer = g + 4 - 8 * y
    low, high = slice(0, half), slice(half, columns)

    def order(step):
        result = jnp.int32(0)
        for plane in range(planes):
            near = sorted(range(planes), key=lambda q: abs(q - plane))
            for at, q in enumerate(near):
                result = result + jnp.where(jnp.logical_and(p == plane, step == at), q, 0)
        return result

    load_v = pltpu.make_async_copy(v_ref, v_in, v_sem)
    load_v.start()

    barrier = pltpu.get_barrier_semaphore()
    for peer in (sibling, x_peer, y_peer):
        pl.semaphore_signal(barrier, inc=1, device_id={"intg": peer}, device_id_type=MESH)

    @pl.when(p > 0)
    def _():
        pl.semaphore_signal(barrier, inc=1, device_id={"pair": p - 1}, device_id_type=MESH)

    @pl.when(p < last)
    def _():
        pl.semaphore_signal(barrier, inc=1, device_id={"pair": p + 1}, device_id_type=MESH)

    ends = (p == 0).astype(jnp.int32) + (p == last).astype(jnp.int32)
    pl.semaphore_wait(barrier, 5 - ends)

    def remote(src, dst, send, recv, **where):
        return pltpu.make_async_remote_copy(
            src_ref=src, dst_ref=dst, send_sem=send, recv_sem=recv,
            device_id=where, device_id_type=MESH,
        )

    def t_copy(src, q, c, send, plane):
        return remote(src, tall.at[q, :, c], send.at[q, c], t_recv.at[q, c], pair=plane)

    def own_t(c):
        @pl.when(p < last)
        def _():
            t_copy(t_ref.at[:, c], p, c, t_right, p + 1).start()

        @pl.when(p > 0)
        def _():
            t_copy(t_ref.at[:, c], p, c, t_left, p - 1).start()

    own_t(0)

    load_v.wait()
    for t in range(tiles):
        span = slice(t * tile, (t + 1) * tile)
        kept = v_in[span, :] * mask_ref[t : t + 1, :]
        turned[span, :] = jnp.dot(
            turn_ref[t], kept, preferred_element_type=jnp.float32
        ).astype(jnp.bfloat16)

    def core_copy(q, c):
        return remote(
            prod.at[q, 1 - core, c], from_core.at[q, c],
            core_send.at[q, c], core_recv.at[q, c], intg=sibling,
        )

    def a_copy(q, c):
        return remote(prod.at[q, core, c, :, low], hop_one.at[q, c, :, low],
                      a_send.at[q, c], a_recv.at[q, c], intg=x_peer)

    def b_copy(q, c):
        return remote(prod.at[q, core, c, :, high], hop_one.at[q, c, :, high],
                      b_send.at[q, c], b_recv.at[q, c], intg=y_peer)

    def a2_copy(q, c):
        return remote(prod.at[q, core, c, :, low], hop_two.at[c, :, low],
                      a2_send.at[c], a2_recv.at[c], intg=y_peer)

    def b2_copy(q, c):
        return remote(prod.at[q, core, c, :, high], hop_two.at[c, :, high],
                      b2_send.at[c], b2_recv.at[c], intg=x_peer)

    events = planes * parts

    def multiply(n):
        c, at = n // planes, n % planes
        q = order(at)

        @pl.when(at == 0)
        def _():
            tall[q, :, c] = t_ref[:, c]

        @pl.when(at > 0)
        def _():
            t_copy(t_ref.at[:, c], q, c, t_right, p).wait_recv()

            @pl.when(jnp.logical_and(q < p, p < last))
            def _():
                t_copy(tall.at[q, :, c], q, c, t_right, p + 1).start()

            @pl.when(jnp.logical_and(q > p, p > 0))
            def _():
                t_copy(tall.at[q, :, c], q, c, t_left, p - 1).start()

        @pl.when(jnp.logical_and(at == 1, c + 1 < parts))
        def _():
            own_t(c + 1)

        left = tall[q, :, c].reshape(CORES * rows, depth)
        wide = min(256, columns)

        def block(i, _):
            span = pl.ds(pl.multiple_of(i * wide, wide), wide)
            prod[q, :, c, :, span] = contract_pair(left, turned[span, :]).reshape(CORES, rows, wide)
            return 0

        lax.fori_loop(0, columns // wide, block, 0)
        core_copy(q, c).start()

    def add_cores(n):
        c, q = n // planes, order(n % planes)
        core_copy(q, c).wait_recv()
        prod[q, core, c] = prod[q, core, c] + from_core[q, c]

        @pl.when(q % 2 != x)
        def _():
            a_copy(q, c).start()

        @pl.when(q // 2 != y)
        def _():
            b_copy(q, c).start()

    def add_first(n):
        c, q = n // planes, order(n % planes)

        @pl.when(q % 2 == x)
        def _():
            a_copy(q, c).wait_recv()
            prod[q, core, c, :, low] = prod[q, core, c, :, low] + hop_one[q, c, :, low]

            @pl.when(q // 2 != y)
            def _():
                a2_copy(q, c).start()

        @pl.when(q // 2 == y)
        def _():
            b_copy(q, c).wait_recv()
            prod[q, core, c, :, high] = prod[q, core, c, :, high] + hop_one[q, c, :, high]

            @pl.when(q % 2 != x)
            def _():
                b2_copy(q, c).start()

    def event(n, _):
        @pl.when(n < events)
        def _():
            multiply(n)

        @pl.when(jnp.logical_and(n >= 1, n < events + 1))
        def _():
            add_cores(n - 1)

        @pl.when(n >= 2)
        def _():
            add_first(n - 2)

        return 0

    lax.fori_loop(0, events + 2, event, 0)

    def right_sum(q, c):
        return remote(cont.at[q, c], from_left.at[q, c], zr_send.at[q, c], zr_recv.at[q, c], pair=p + 1)

    def left_sum(q, c):
        return remote(cont.at[q, c], from_right.at[q, c], zl_send.at[q, c], zl_recv.at[q, c], pair=p - 1)

    def collect(c):
        a2_copy(chip, c).wait_recv()
        b2_copy(chip, c).wait_recv()
        prod[chip, core, c] = prod[chip, core, c] + hop_two[c]

        def fill(q):
            for s in range(per_plane):
                def term(t, total):
                    span = pl.ds(pl.multiple_of(t * tile, tile), tile)
                    scale = pick_ref[(q * per_plane + s) * tiles + t]
                    return total + scale * prod[chip, core, c, :, span]

                cont[q, c, :, s * tile : (s + 1) * tile] = lax.fori_loop(
                    0, tiles, term, jnp.zeros((rows, tile), jnp.float32))

        for away in range(last, 0, -1):
            @pl.when(p + away <= last)
            def _():
                q = p + away
                fill(q)

                @pl.when(p > 0)
                def _():
                    right_sum(q, c).wait_recv()
                    cont[q, c] = cont[q, c] + from_left[q, c]

                right_sum(q, c).start()

            @pl.when(p - away >= 0)
            def _():
                q = p - away
                fill(q)

                @pl.when(p < last)
                def _():
                    left_sum(q, c).wait_recv()
                    cont[q, c] = cont[q, c] + from_right[q, c]

                left_sum(q, c).start()
        fill(p)

    def right_slot(q, c):
        return remote(slots.at[q, c], slots.at[q, c], gr_send.at[q, c], g_recv.at[q, c], pair=p + 1)

    def left_slot(q, c):
        return remote(slots.at[q, c], slots.at[q, c], gl_send.at[q, c], g_recv.at[q, c], pair=p - 1)

    def settle(c):
        @pl.when(p > 0)
        def _():
            right_sum(p, c).wait_recv()
            cont[p, c] = cont[p, c] + from_left[p, c]

        @pl.when(p < last)
        def _():
            left_sum(p, c).wait_recv()
            cont[p, c] = cont[p, c] + from_right[p, c]

        slots[p, c] = cont[p, c].astype(jnp.bfloat16)

        @pl.when(p < last)
        def _():
            right_slot(p, c).start()

        @pl.when(p > 0)
        def _():
            left_slot(p, c).start()

    def pass_on(c):
        for away in range(1, planes):
            @pl.when(p - away >= 0)
            def _():
                q = p - away
                right_slot(q, c).wait_recv()

                @pl.when(p < last)
                def _():
                    right_slot(q, c).start()

            @pl.when(p + away <= last)
            def _():
                q = p + away
                left_slot(q, c).wait_recv()

                @pl.when(p > 0)
                def _():
                    left_slot(q, c).start()

    def emit(c):
        def one(t, _):
            total = jnp.zeros((rows, tile), jnp.float32)
            for q in range(planes):
                for s in range(per_plane):
                    scale = pick_ref[(q * per_plane + s) * tiles + t]
                    total = total + scale * slots[q, c, :, s * tile : (s + 1) * tile].astype(jnp.float32)
            span = pl.ds(pl.multiple_of(t * tile, tile), tile)
            out_ref[c * rows : (c + 1) * rows, span] = jnp.dot(
                total.astype(jnp.bfloat16), turn_ref[t], preferred_element_type=jnp.float32
            ).astype(jnp.bfloat16)
            return 0

        lax.fori_loop(0, tiles, one, 0)

    for c in range(parts):
        collect(c)
    for c in range(parts):
        settle(c)
    for c in range(parts):
        pass_on(c)
        emit(c)

    def drain(n, _):
        c, q = n // planes, n % planes
        core_copy(q, c).wait_send()

        @pl.when(q % 2 != x)
        def _():
            a_copy(q, c).wait_send()

        @pl.when(q // 2 != y)
        def _():
            b_copy(q, c).wait_send()

        @pl.when(jnp.logical_and(q % 2 == x, q // 2 != y))
        def _():
            a2_copy(q, c).wait_send()

        @pl.when(jnp.logical_and(q % 2 != x, q // 2 == y))
        def _():
            b2_copy(q, c).wait_send()

        @pl.when(jnp.logical_and(q <= p, p < last))
        def _():
            t_copy(tall.at[q, :, c], q, c, t_right, p + 1).wait_send()
            right_slot(q, c).wait_send()

        @pl.when(jnp.logical_and(q >= p, p > 0))
        def _():
            t_copy(tall.at[q, :, c], q, c, t_left, p - 1).wait_send()
            left_slot(q, c).wait_send()

        @pl.when(q > p)
        def _():
            right_sum(q, c).wait_send()

        @pl.when(q < p)
        def _():
            left_sum(q, c).wait_send()

        return 0

    lax.fori_loop(0, events, drain, 0)


def shards(planes, amplitudes, integrals, sym_rows, sym_cols, mirror_rows):
    tiles = sym_rows.shape[0]
    columns, depth = integrals.shape
    tile = columns // tiles
    all_tiles = mirror_rows.shape[0] // tile
    count = all_tiles // 2
    per_plane = count // planes
    rows = amplitudes.shape[0] // (CORES * PARTS)

    mask = (sym_rows[:, None] == jnp.repeat(sym_cols, tile)[None, :]).astype(jnp.bfloat16)
    twin = mirror_rows.reshape(all_tiles, tile)
    partner = twin[:, 0] // tile
    here = jnp.arange(all_tiles, dtype=jnp.int32)
    leads = here < partner
    first = jnp.minimum(here, partner)
    rank = jnp.sum((leads[None, :]) & (here[None, :] < first[:, None]), axis=1).astype(jnp.int32)
    start = lax.axis_index("pair") * tiles
    own_twin = lax.dynamic_slice_in_dim(twin, start, tiles, 0) % tile
    own_leads = lax.dynamic_slice_in_dim(leads, start, tiles, 0)
    own_rank = lax.dynamic_slice_in_dim(rank, start, tiles, 0)
    lane = jnp.arange(tile, dtype=jnp.int32)
    spot = jnp.where(own_leads[:, None], lane[None, :], own_twin)
    sign = jnp.where(own_leads, 1.0, -1.0).astype(jnp.bfloat16)
    turn = jnp.where(lane[None, :, None] == spot[:, None, :], sign[:, None, None], jnp.zeros((), jnp.bfloat16))
    pick = (jnp.arange(count, dtype=jnp.int32)[:, None] == own_rank[None, :]).astype(jnp.float32).reshape(-1)

    dma = pltpu.SemaphoreType.DMA
    grid = (planes, PARTS)
    vmem = pl.BlockSpec(memory_space=pltpu.VMEM)
    group = per_plane * tile
    return pl.pallas_call(
        functools.partial(ladder_kernel, planes, tiles, tile),
        out_shape=jax.ShapeDtypeStruct((PARTS * rows, columns), jnp.bfloat16),
        in_specs=[vmem, pl.BlockSpec(memory_space=pl.ANY), vmem, vmem, pl.BlockSpec(memory_space=pltpu.SMEM)],
        out_specs=vmem,
        scratch_shapes=[
            pltpu.VMEM((columns, depth), jnp.bfloat16),
            pltpu.VMEM((columns, depth), jnp.bfloat16),
            pltpu.VMEM((planes, CORES, PARTS, rows, depth), jnp.bfloat16),
            pltpu.VMEM((planes, CORES, PARTS, rows, columns), jnp.float32),
            pltpu.VMEM((planes, PARTS, rows, columns), jnp.float32),
            pltpu.VMEM((planes, PARTS, rows, columns), jnp.float32),
            pltpu.VMEM((PARTS, rows, columns), jnp.float32),
            pltpu.VMEM((planes, PARTS, rows, group), jnp.float32),
            pltpu.VMEM((planes, PARTS, rows, group), jnp.float32),
            pltpu.VMEM((planes, PARTS, rows, group), jnp.float32),
            pltpu.VMEM((planes, PARTS, rows, group), jnp.bfloat16),
            dma,
            dma(grid), dma(grid), dma(grid), dma(grid), dma(grid),
            dma(grid), dma(grid), dma(grid), dma(grid),
            dma((PARTS,)), dma((PARTS,)), dma((PARTS,)), dma((PARTS,)),
            dma(grid), dma(grid), dma(grid), dma(grid),
            dma(grid), dma(grid), dma(grid),
        ],
        compiler_params=pltpu.CompilerParams(
            collective_id=0, has_side_effects=True, vmem_limit_bytes=48 * 1024 * 1024
        ),
        cost_estimate=pl.CostEstimate(
            flops=2 * planes * amplitudes.shape[0] * columns * depth,
            bytes_accessed=2 * (amplitudes.size + integrals.size), transcendentals=0,
        ),
    )(amplitudes.reshape(CORES, PARTS, rows, depth), integrals, mask, turn, pick)


def solution(mesh):
    planes, chips = mesh.shape["pair"], mesh.shape["intg"] // CORES
    direct = planes == chips and chips == SIDE * SIDE
    body = functools.partial(shards, planes) if direct else shards_plain
    return jax.shard_map(
        body,
        mesh=mesh,
        in_specs=(P("pair", "intg"), P("pair", "intg"), P("pair"), P("intg"), P()),
        out_specs=P("intg", "pair"),
        check_vma=False,
    )
```

```python
import functools

import jax
import jax.numpy as jnp
from jax import lax
from jax.experimental import pallas as pl
from jax.experimental.pallas import tpu as pltpu
from jax.sharding import PartitionSpec as P

MESH = pl.DeviceIdType.MESH
PARTS = 4
LAG = 3
CORES = 2
SIDE = 2


def contract_pair(left, right):
    return lax.dot_general(
        left, right, (((1,), (1,)), ((), ())), preferred_element_type=jnp.float32
    )


def shards_plain(amplitudes, integrals, sym_rows, sym_cols, mirror_rows):
    tile_rows = integrals.shape[0] // sym_rows.shape[0]
    row_sym = jnp.repeat(sym_rows, tile_rows)
    col_sym = jnp.repeat(sym_cols, tile_rows)
    masked = jnp.where(row_sym[:, None] == col_sym[None, :], integrals, jnp.zeros((), jnp.bfloat16))
    ab_rows = integrals.shape[0]
    own_twins = lax.dynamic_slice_in_dim(mirror_rows, lax.axis_index("pair") * ab_rows, ab_rows, 0)
    partial_sums = contract_pair(lax.all_gather(amplitudes, "pair", axis=0, tiled=True), masked)
    result_block = lax.psum_scatter(partial_sums, "intg", scatter_dimension=0, tiled=True)
    all_columns = lax.all_gather(result_block, "pair", axis=1, tiled=True)
    result_block = result_block - jnp.take(all_columns, own_twins, axis=1)
    return result_block.astype(jnp.bfloat16)


def ladder_kernel(
    planes, tiles, tile,
    t_ref, v_ref, rows_ref, cols_ref, mirror_ref, twin_ref, out_ref,
    rank_ref, turn, v_in, turned, tall, prod, from_core, hop_one, hop_two, cont, from_left, from_right, slots,
    v_sem, own_sem, t_recv, t_right, t_left, core_send, core_recv,
    a_send, a_recv, b_send, b_recv, a2_send, a2_recv, b2_send, b2_recv,
    zr_send, zr_recv, zl_send, zl_recv, gr_send, gl_send, g_recv,
):
    parts, rows, depth = t_ref.shape[1], t_ref.shape[2], t_ref.shape[3]
    columns = prod.shape[-1]
    half = columns // 2
    group = cont.shape[-1]
    per_plane = group // tile
    last = planes - 1
    p = lax.axis_index("pair")
    g = lax.axis_index("intg")
    core, x, y = g % 2, (g // 2) % 2, g // 4
    chip = g // 2
    sibling = g + 1 - 2 * core
    x_peer = g + 2 - 4 * x
    y_peer = g + 4 - 8 * y
    low, high = slice(0, half), slice(half, columns)

    def order(step):
        result = jnp.int32(0)
        for plane in range(planes):
            near = sorted(range(planes), key=lambda q: abs(q - plane))
            for at, q in enumerate(near):
                result = result + jnp.where(jnp.logical_and(p == plane, step == at), q, 0)
        return result

    load_v = pltpu.make_async_copy(v_ref, v_in, v_sem)
    load_v.start()
    load_t = pltpu.make_async_copy(t_ref, tall.at[p], own_sem)
    load_t.start()

    barrier = pltpu.get_barrier_semaphore()
    for peer in (sibling, x_peer, y_peer):
        pl.semaphore_signal(barrier, inc=1, device_id={"intg": peer}, device_id_type=MESH)

    @pl.when(p > 0)
    def _():
        pl.semaphore_signal(barrier, inc=1, device_id={"pair": p - 1}, device_id_type=MESH)

    @pl.when(p < last)
    def _():
        pl.semaphore_signal(barrier, inc=1, device_id={"pair": p + 1}, device_id_type=MESH)

    ends = (p == 0).astype(jnp.int32) + (p == last).astype(jnp.int32)
    pl.semaphore_wait(barrier, 5 - ends)

    def remote(src, dst, send, recv, **where):
        return pltpu.make_async_remote_copy(
            src_ref=src, dst_ref=dst, send_sem=send, recv_sem=recv,
            device_id=where, device_id_type=MESH,
        )

    def t_copy(src, q, c, send, plane):
        return remote(src, tall.at[q, :, c], send.at[q, c], t_recv.at[q, c], pair=plane)

    def own_t(c):
        @pl.when(p < last)
        def _():
            t_copy(t_ref.at[:, c], p, c, t_right, p + 1).start()

        @pl.when(p > 0)
        def _():
            t_copy(t_ref.at[:, c], p, c, t_left, p - 1).start()

    own_t(0)

    all_tiles = planes * tiles
    base = p * tiles
    partners = [mirror_ref[u * tile] // tile for u in range(all_tiles)]
    load_v.wait()

    def prepare(t, _):
        at = base + t
        partner = mirror_ref[at * tile] // tile
        leads = at < partner
        first = jnp.minimum(at, partner)
        rank = jnp.int32(0)
        for u in range(all_tiles):
            rank = rank + jnp.where(jnp.logical_and(u < partners[u], u < first), 1, 0)
        rank_ref[t] = rank
        lane = lax.broadcasted_iota(jnp.int32, (1, tile), 1)
        spot = jnp.where(leads, lane, twin_ref[pl.ds(at, 1), :] - partner * tile)
        sign = jnp.where(leads, 1.0, -1.0)
        row = lax.broadcasted_iota(jnp.int32, (tile, tile), 0)
        turn[t] = jnp.where(row == spot, sign, 0.0).astype(jnp.bfloat16)
        span = pl.ds(pl.multiple_of(t * tile, tile), tile)
        for u in range(depth // tile):
            keep = jnp.where(rows_ref[t] == cols_ref[u], 1.0, 0.0)
            lanes = slice(u * tile, (u + 1) * tile)
            v_in[span, lanes] = (v_in[span, lanes].astype(jnp.float32) * keep).astype(jnp.bfloat16)
        turned[span, :] = jnp.dot(
            turn[t], v_in[span, :], preferred_element_type=jnp.float32
        ).astype(jnp.bfloat16)
        return 0

    lax.fori_loop(0, tiles, prepare, 0)
    load_t.wait()

    def core_copy(q, c):
        return remote(
            prod.at[q, 1 - core, c], from_core.at[q, c],
            core_send.at[q, c], core_recv.at[q, c], intg=sibling,
        )

    def a_copy(q, c):
        return remote(prod.at[q, core, c, :, low], hop_one.at[q, c, :, low],
                      a_send.at[q, c], a_recv.at[q, c], intg=x_peer)

    def b_copy(q, c):
        return remote(prod.at[q, core, c, :, high], hop_one.at[q, c, :, high],
                      b_send.at[q, c], b_recv.at[q, c], intg=y_peer)

    def a2_copy(q, c):
        return remote(prod.at[q, core, c, :, low], hop_two.at[c, :, low],
                      a2_send.at[c], a2_recv.at[c], intg=y_peer)

    def b2_copy(q, c):
        return remote(prod.at[q, core, c, :, high], hop_two.at[c, :, high],
                      b2_send.at[c], b2_recv.at[c], intg=x_peer)

    events = planes * parts

    def multiply(n):
        c, at = n // planes, n % planes
        q = order(at)

        @pl.when(at > 0)
        def _():
            t_copy(t_ref.at[:, c], q, c, t_right, p).wait_recv()

            @pl.when(jnp.logical_and(q < p, p < last))
            def _():
                t_copy(tall.at[q, :, c], q, c, t_right, p + 1).start()

            @pl.when(jnp.logical_and(q > p, p > 0))
            def _():
                t_copy(tall.at[q, :, c], q, c, t_left, p - 1).start()

        @pl.when(jnp.logical_and(at == 1, c + 1 < parts))
        def _():
            own_t(c + 1)

        left = tall[q, :, c].reshape(CORES * rows, depth)
        wide = min(256, columns)

        def block(i, _):
            span = pl.ds(pl.multiple_of(i * wide, wide), wide)
            prod[q, :, c, :, span] = contract_pair(left, turned[span, :]).reshape(CORES, rows, wide)
            return 0

        lax.fori_loop(0, columns // wide, block, 0)
        core_copy(q, c).start()

    def add_cores(n):
        c, q = n // planes, order(n % planes)
        core_copy(q, c).wait_recv()
        prod[q, core, c] = prod[q, core, c] + from_core[q, c]

        @pl.when(q % 2 != x)
        def _():
            a_copy(q, c).start()

        @pl.when(q // 2 != y)
        def _():
            b_copy(q, c).start()

    def add_first(n):
        c, q = n // planes, order(n % planes)

        @pl.when(q % 2 == x)
        def _():
            a_copy(q, c).wait_recv()
            prod[q, core, c, :, low] = prod[q, core, c, :, low] + hop_one[q, c, :, low]

            @pl.when(q // 2 != y)
            def _():
                a2_copy(q, c).start()

        @pl.when(q // 2 == y)
        def _():
            b_copy(q, c).wait_recv()
            prod[q, core, c, :, high] = prod[q, core, c, :, high] + hop_one[q, c, :, high]

            @pl.when(q % 2 != x)
            def _():
                b2_copy(q, c).start()

    def right_sum(q, c):
        return remote(cont.at[q, c], from_left.at[q, c], zr_send.at[q, c], zr_recv.at[q, c], pair=p + 1)

    def left_sum(q, c):
        return remote(cont.at[q, c], from_right.at[q, c], zl_send.at[q, c], zl_recv.at[q, c], pair=p - 1)

    def pick(k, t):
        return jnp.where(rank_ref[t] == k, 1.0, 0.0)

    def collect(c):
        a2_copy(chip, c).wait_recv()
        b2_copy(chip, c).wait_recv()
        prod[chip, core, c] = prod[chip, core, c] + hop_two[c]

        def fill(k, _):
            total = jnp.zeros((rows, tile), jnp.float32)
            for t in range(tiles):
                total = total + pick(k, t) * prod[chip, core, c, :, t * tile : (t + 1) * tile]
            span = pl.ds(pl.multiple_of(k % per_plane * tile, tile), tile)
            cont[k // per_plane, c, :, span] = total
            return 0

        lax.fori_loop(0, planes * per_plane, fill, 0)
        send_sums(c, last)

    def send_sums(c, away):
        @pl.when(p + away <= last)
        def _():
            q = p + away

            @pl.when(p > 0)
            def _():
                right_sum(q, c).wait_recv()
                cont[q, c] = cont[q, c] + from_left[q, c]

            right_sum(q, c).start()

        @pl.when(p - away >= 0)
        def _():
            q = p - away

            @pl.when(p < last)
            def _():
                left_sum(q, c).wait_recv()
                cont[q, c] = cont[q, c] + from_right[q, c]

            left_sum(q, c).start()

    def right_slot(q, c):
        return remote(slots.at[q, c], slots.at[q, c], gr_send.at[q, c], g_recv.at[q, c], pair=p + 1)

    def left_slot(q, c):
        return remote(slots.at[q, c], slots.at[q, c], gl_send.at[q, c], g_recv.at[q, c], pair=p - 1)

    def settle(c):
        @pl.when(p > 0)
        def _():
            right_sum(p, c).wait_recv()
            cont[p, c] = cont[p, c] + from_left[p, c]

        @pl.when(p < last)
        def _():
            left_sum(p, c).wait_recv()
            cont[p, c] = cont[p, c] + from_right[p, c]

        slots[p, c] = cont[p, c].astype(jnp.bfloat16)

        @pl.when(p < last)
        def _():
            right_slot(p, c).start()

        @pl.when(p > 0)
        def _():
            left_slot(p, c).start()

    def pass_on(c, away):
        @pl.when(p - away >= 0)
        def _():
            q = p - away
            right_slot(q, c).wait_recv()

            @pl.when(p < last)
            def _():
                right_slot(q, c).start()

        @pl.when(p + away <= last)
        def _():
            q = p + away
            left_slot(q, c).wait_recv()

            @pl.when(p > 0)
            def _():
                left_slot(q, c).start()

    def emit(c):
        def one(t, _):
            total = jnp.zeros((rows, tile), jnp.float32)
            for q in range(planes):
                for s in range(per_plane):
                    scale = pick(q * per_plane + s, t)
                    total = total + scale * slots[q, c, :, s * tile : (s + 1) * tile].astype(jnp.float32)
            span = pl.ds(pl.multiple_of(t * tile, tile), tile)
            out_ref[pl.ds(pl.multiple_of(c * rows, rows), rows), span] = jnp.dot(
                total.astype(jnp.bfloat16), turn[t], preferred_element_type=jnp.float32
            ).astype(jnp.bfloat16)
            return 0

        lax.fori_loop(0, tiles, one, 0)

    stages = [collect]
    stages += [functools.partial(send_sums, away=away) for away in range(last - 1, 0, -1)]
    stages += [settle]
    stages += [functools.partial(pass_on, away=away) for away in range(1, planes)]
    stages += [emit]

    def event(n, _):
        @pl.when(n < events)
        def _():
            multiply(n)

        @pl.when(jnp.logical_and(n >= 1, n < events + 1))
        def _():
            add_cores(n - 1)

        @pl.when(jnp.logical_and(n >= 2, n < events + 2))
        def _():
            add_first(n - 2)

        for at, stage in enumerate(stages):
            since = n - planes - LAG - at
            c = jnp.maximum(since, 0) // planes

            @pl.when(jnp.logical_and(jnp.logical_and(since >= 0, c < parts), since % planes == 0))
            def _():
                stage(c)

        return 0

    lax.fori_loop(0, events + LAG + len(stages), event, 0)

    def drain(n, _):
        c, q = n // planes, n % planes
        core_copy(q, c).wait_send()

        @pl.when(q % 2 != x)
        def _():
            a_copy(q, c).wait_send()

        @pl.when(q // 2 != y)
        def _():
            b_copy(q, c).wait_send()

        @pl.when(jnp.logical_and(q % 2 == x, q // 2 != y))
        def _():
            a2_copy(q, c).wait_send()

        @pl.when(jnp.logical_and(q % 2 != x, q // 2 == y))
        def _():
            b2_copy(q, c).wait_send()

        @pl.when(jnp.logical_and(q <= p, p < last))
        def _():
            t_copy(tall.at[q, :, c], q, c, t_right, p + 1).wait_send()
            right_slot(q, c).wait_send()

        @pl.when(jnp.logical_and(q >= p, p > 0))
        def _():
            t_copy(tall.at[q, :, c], q, c, t_left, p - 1).wait_send()
            left_slot(q, c).wait_send()

        @pl.when(q > p)
        def _():
            right_sum(q, c).wait_send()

        @pl.when(q < p)
        def _():
            left_sum(q, c).wait_send()

        return 0

    lax.fori_loop(0, events, drain, 0)


def shards(planes, amplitudes, integrals, sym_rows, sym_cols, mirror_rows):
    tiles = sym_rows.shape[0]
    columns, depth = integrals.shape
    tile = columns // tiles
    all_tiles = mirror_rows.shape[0] // tile
    per_plane = all_tiles // 2 // planes
    rows = amplitudes.shape[0] // (CORES * PARTS)

    dma = pltpu.SemaphoreType.DMA
    grid = (planes, PARTS)
    vmem = pl.BlockSpec(memory_space=pltpu.VMEM)
    smem = pl.BlockSpec(memory_space=pltpu.SMEM)
    hbm = pl.BlockSpec(memory_space=pl.ANY)
    group = per_plane * tile
    return pl.pallas_call(
        functools.partial(ladder_kernel, planes, tiles, tile),
        out_shape=jax.ShapeDtypeStruct((PARTS * rows, columns), jnp.bfloat16),
        in_specs=[hbm, hbm, smem, smem, smem, vmem],
        out_specs=vmem,
        scratch_shapes=[
            pltpu.SMEM((tiles,), jnp.int32),
            pltpu.VMEM((tiles, tile, tile), jnp.bfloat16),
            pltpu.VMEM((columns, depth), jnp.bfloat16),
            pltpu.VMEM((columns, depth), jnp.bfloat16),
            pltpu.VMEM((planes, CORES, PARTS, rows, depth), jnp.bfloat16),
            pltpu.VMEM((planes, CORES, PARTS, rows, columns), jnp.float32),
            pltpu.VMEM((planes, PARTS, rows, columns), jnp.float32),
            pltpu.VMEM((planes, PARTS, rows, columns), jnp.float32),
            pltpu.VMEM((PARTS, rows, columns), jnp.float32),
            pltpu.VMEM((planes, PARTS, rows, group), jnp.float32),
            pltpu.VMEM((planes, PARTS, rows, group), jnp.float32),
            pltpu.VMEM((planes, PARTS, rows, group), jnp.float32),
            pltpu.VMEM((planes, PARTS, rows, group), jnp.bfloat16),
            dma, dma,
            dma(grid), dma(grid), dma(grid), dma(grid), dma(grid),
            dma(grid), dma(grid), dma(grid), dma(grid),
            dma((PARTS,)), dma((PARTS,)), dma((PARTS,)), dma((PARTS,)),
            dma(grid), dma(grid), dma(grid), dma(grid),
            dma(grid), dma(grid), dma(grid),
        ],
        compiler_params=pltpu.CompilerParams(
            collective_id=0, has_side_effects=True, vmem_limit_bytes=48 * 1024 * 1024
        ),
        cost_estimate=pl.CostEstimate(
            flops=2 * planes * amplitudes.shape[0] * columns * depth,
            bytes_accessed=2 * (amplitudes.size + integrals.size), transcendentals=0,
        ),
    )(amplitudes.reshape(CORES, PARTS, rows, depth), integrals, sym_rows, sym_cols,
      mirror_rows, mirror_rows.reshape(all_tiles, tile))


def solution(mesh):
    planes, chips = mesh.shape["pair"], mesh.shape["intg"] // CORES
    direct = planes == chips and chips == SIDE * SIDE
    body = functools.partial(shards, planes) if direct else shards_plain
    return jax.shard_map(
        body,
        mesh=mesh,
        in_specs=(P("pair", "intg"), P("pair", "intg"), P("pair"), P("intg"), P()),
        out_specs=P("intg", "pair"),
        check_vma=False,
    )
```

```python
import functools

import jax
import jax.numpy as jnp
from jax import lax
from jax.experimental import pallas as pl
from jax.experimental.pallas import tpu as pltpu
from jax.sharding import PartitionSpec as P

MESH = pl.DeviceIdType.MESH
PARTS = 4
LAG = 3
AHEAD = 2
CORES = 2
SIDE = 2


def contract_pair(left, right):
    return lax.dot_general(
        left, right, (((1,), (1,)), ((), ())), preferred_element_type=jnp.float32
    )


def shards_plain(amplitudes, integrals, sym_rows, sym_cols, mirror_rows):
    tile_rows = integrals.shape[0] // sym_rows.shape[0]
    row_sym = jnp.repeat(sym_rows, tile_rows)
    col_sym = jnp.repeat(sym_cols, tile_rows)
    masked = jnp.where(row_sym[:, None] == col_sym[None, :], integrals, jnp.zeros((), jnp.bfloat16))
    ab_rows = integrals.shape[0]
    own_twins = lax.dynamic_slice_in_dim(mirror_rows, lax.axis_index("pair") * ab_rows, ab_rows, 0)
    partial_sums = contract_pair(lax.all_gather(amplitudes, "pair", axis=0, tiled=True), masked)
    result_block = lax.psum_scatter(partial_sums, "intg", scatter_dimension=0, tiled=True)
    all_columns = lax.all_gather(result_block, "pair", axis=1, tiled=True)
    result_block = result_block - jnp.take(all_columns, own_twins, axis=1)
    return result_block.astype(jnp.bfloat16)


def ladder_kernel(
    planes, tiles, tile,
    t_ref, v_ref, rows_ref, cols_ref, mirror_ref, twin_ref, out_ref,
    rank_ref, turn, v_in, turned, tall, prod, from_core, hop_one, hop_two, cont, from_left, from_right, slots,
    v_sem, own_sem, t_recv, t_right, t_left, core_send, core_recv,
    a_send, a_recv, b_send, b_recv, a2_send, a2_recv, b2_send, b2_recv,
    zr_send, zr_recv, zl_send, zl_recv, gr_send, gl_send, g_recv,
):
    parts, rows, depth = t_ref.shape[1], t_ref.shape[2], t_ref.shape[3]
    columns = prod.shape[-1]
    half = columns // 2
    group = cont.shape[-1]
    per_plane = group // tile
    last = planes - 1
    p = lax.axis_index("pair")
    g = lax.axis_index("intg")
    core, x, y = g % 2, (g // 2) % 2, g // 4
    chip = g // 2
    sibling = g + 1 - 2 * core
    x_peer = g + 2 - 4 * x
    y_peer = g + 4 - 8 * y
    low, high = slice(0, half), slice(half, columns)

    def order(step):
        result = jnp.int32(0)
        for plane in range(planes):
            near = sorted(range(planes), key=lambda q: abs(q - plane))
            for at, q in enumerate(near):
                result = result + jnp.where(jnp.logical_and(p == plane, step == at), q, 0)
        return result

    load_v = pltpu.make_async_copy(v_ref, v_in, v_sem)
    load_v.start()
    load_t = pltpu.make_async_copy(t_ref, tall.at[p], own_sem)
    load_t.start()

    barrier = pltpu.get_barrier_semaphore()
    for peer in (sibling, x_peer, y_peer):
        pl.semaphore_signal(barrier, inc=1, device_id={"intg": peer}, device_id_type=MESH)

    @pl.when(p > 0)
    def _():
        pl.semaphore_signal(barrier, inc=1, device_id={"pair": p - 1}, device_id_type=MESH)

    @pl.when(p < last)
    def _():
        pl.semaphore_signal(barrier, inc=1, device_id={"pair": p + 1}, device_id_type=MESH)

    ends = (p == 0).astype(jnp.int32) + (p == last).astype(jnp.int32)
    pl.semaphore_wait(barrier, 5 - ends)

    def remote(src, dst, send, recv, **where):
        return pltpu.make_async_remote_copy(
            src_ref=src, dst_ref=dst, send_sem=send, recv_sem=recv,
            device_id=where, device_id_type=MESH,
        )

    def t_copy(src, q, c, send, plane):
        return remote(src, tall.at[q, :, c], send.at[q, c], t_recv.at[q, c], pair=plane)

    def own_t(c):
        @pl.when(p < last)
        def _():
            t_copy(t_ref.at[:, c], p, c, t_right, p + 1).start()

        @pl.when(p > 0)
        def _():
            t_copy(t_ref.at[:, c], p, c, t_left, p - 1).start()

    for c in range(AHEAD):
        own_t(c)

    all_tiles = planes * tiles
    base = p * tiles
    partners = [mirror_ref[u * tile] // tile for u in range(all_tiles)]
    load_v.wait()

    def prepare(t, _):
        at = base + t
        partner = mirror_ref[at * tile] // tile
        leads = at < partner
        first = jnp.minimum(at, partner)
        rank = jnp.int32(0)
        for u in range(all_tiles):
            rank = rank + jnp.where(jnp.logical_and(u < partners[u], u < first), 1, 0)
        rank_ref[t] = rank
        lane = lax.broadcasted_iota(jnp.int32, (1, tile), 1)
        spot = jnp.where(leads, lane, twin_ref[pl.ds(at, 1), :] - partner * tile)
        sign = jnp.where(leads, 1.0, -1.0)
        row = lax.broadcasted_iota(jnp.int32, (tile, tile), 0)
        turn[t] = jnp.where(row == spot, sign, 0.0).astype(jnp.bfloat16)
        span = pl.ds(pl.multiple_of(t * tile, tile), tile)
        for u in range(depth // tile):
            keep = jnp.where(rows_ref[t] == cols_ref[u], 1.0, 0.0)
            lanes = slice(u * tile, (u + 1) * tile)
            v_in[span, lanes] = (v_in[span, lanes].astype(jnp.float32) * keep).astype(jnp.bfloat16)
        turned[:, span] = jnp.dot(
            turn[t], v_in[span, :], preferred_element_type=jnp.float32
        ).T.astype(jnp.bfloat16)
        return 0

    lax.fori_loop(0, tiles, prepare, 0)
    load_t.wait()

    def core_copy(q, c):
        return remote(
            prod.at[q, 1 - core, c], from_core.at[q, c],
            core_send.at[q, c], core_recv.at[q, c], intg=sibling,
        )

    def a_copy(q, c):
        return remote(prod.at[q, core, c, :, low], hop_one.at[q, c, :, low],
                      a_send.at[q, c], a_recv.at[q, c], intg=x_peer)

    def b_copy(q, c):
        return remote(prod.at[q, core, c, :, high], hop_one.at[q, c, :, high],
                      b_send.at[q, c], b_recv.at[q, c], intg=y_peer)

    def a2_copy(q, c):
        return remote(prod.at[q, core, c, :, low], hop_two.at[c, :, low],
                      a2_send.at[c], a2_recv.at[c], intg=y_peer)

    def b2_copy(q, c):
        return remote(prod.at[q, core, c, :, high], hop_two.at[c, :, high],
                      b2_send.at[c], b2_recv.at[c], intg=x_peer)

    events = planes * parts

    def multiply(n):
        c, at = n // planes, n % planes
        q = order(at)

        @pl.when(at > 0)
        def _():
            t_copy(t_ref.at[:, c], q, c, t_right, p).wait_recv()

            @pl.when(jnp.logical_and(q < p, p < last))
            def _():
                t_copy(tall.at[q, :, c], q, c, t_right, p + 1).start()

            @pl.when(jnp.logical_and(q > p, p > 0))
            def _():
                t_copy(tall.at[q, :, c], q, c, t_left, p - 1).start()

        @pl.when(jnp.logical_and(at == 1, c + AHEAD < parts))
        def _():
            own_t(c + AHEAD)

        left = tall[q, :, c].reshape(CORES * rows, depth)
        wide = min(256, columns)

        def block(i, _):
            span = pl.ds(pl.multiple_of(i * wide, wide), wide)
            prod[q, :, c, :, span] = jnp.dot(
                left, turned[:, span], preferred_element_type=jnp.float32
            ).reshape(CORES, rows, wide)
            return 0

        lax.fori_loop(0, columns // wide, block, 0)
        core_copy(q, c).start()

    def add_cores(n):
        c, q = n // planes, order(n % planes)
        core_copy(q, c).wait_recv()
        prod[q, core, c] = prod[q, core, c] + from_core[q, c]

        @pl.when(q % 2 != x)
        def _():
            a_copy(q, c).start()

        @pl.when(q // 2 != y)
        def _():
            b_copy(q, c).start()

    def add_first(n):
        c, q = n // planes, order(n % planes)

        @pl.when(q % 2 == x)
        def _():
            a_copy(q, c).wait_recv()
            prod[q, core, c, :, low] = prod[q, core, c, :, low] + hop_one[q, c, :, low]

            @pl.when(q // 2 != y)
            def _():
                a2_copy(q, c).start()

        @pl.when(q // 2 == y)
        def _():
            b_copy(q, c).wait_recv()
            prod[q, core, c, :, high] = prod[q, core, c, :, high] + hop_one[q, c, :, high]

            @pl.when(q % 2 != x)
            def _():
                b2_copy(q, c).start()

    def right_sum(q, c):
        return remote(cont.at[q, c], from_left.at[q, c], zr_send.at[q, c], zr_recv.at[q, c], pair=p + 1)

    def left_sum(q, c):
        return remote(cont.at[q, c], from_right.at[q, c], zl_send.at[q, c], zl_recv.at[q, c], pair=p - 1)

    def pick(k, t):
        return jnp.where(rank_ref[t] == k, 1.0, 0.0)

    def collect(c):
        a2_copy(chip, c).wait_recv()
        b2_copy(chip, c).wait_recv()
        prod[chip, core, c] = prod[chip, core, c] + hop_two[c]

        def fill(k, _):
            total = jnp.zeros((rows, tile), jnp.float32)
            for t in range(tiles):
                total = total + pick(k, t) * prod[chip, core, c, :, t * tile : (t + 1) * tile]
            span = pl.ds(pl.multiple_of(k % per_plane * tile, tile), tile)
            cont[k // per_plane, c, :, span] = total
            return 0

        lax.fori_loop(0, planes * per_plane, fill, 0)
        send_sums(c, last)

    def send_sums(c, away):
        @pl.when(p + away <= last)
        def _():
            q = p + away

            @pl.when(p > 0)
            def _():
                right_sum(q, c).wait_recv()
                cont[q, c] = cont[q, c] + from_left[q, c]

            right_sum(q, c).start()

        @pl.when(p - away >= 0)
        def _():
            q = p - away

            @pl.when(p < last)
            def _():
                left_sum(q, c).wait_recv()
                cont[q, c] = cont[q, c] + from_right[q, c]

            left_sum(q, c).start()

    def right_slot(q, c):
        return remote(slots.at[q, c], slots.at[q, c], gr_send.at[q, c], g_recv.at[q, c], pair=p + 1)

    def left_slot(q, c):
        return remote(slots.at[q, c], slots.at[q, c], gl_send.at[q, c], g_recv.at[q, c], pair=p - 1)

    def settle(c):
        @pl.when(p > 0)
        def _():
            right_sum(p, c).wait_recv()
            cont[p, c] = cont[p, c] + from_left[p, c]

        @pl.when(p < last)
        def _():
            left_sum(p, c).wait_recv()
            cont[p, c] = cont[p, c] + from_right[p, c]

        slots[p, c] = cont[p, c].astype(jnp.bfloat16)

        @pl.when(p < last)
        def _():
            right_slot(p, c).start()

        @pl.when(p > 0)
        def _():
            left_slot(p, c).start()

    def pass_on(c, away):
        @pl.when(p - away >= 0)
        def _():
            q = p - away
            right_slot(q, c).wait_recv()

            @pl.when(p < last)
            def _():
                right_slot(q, c).start()

        @pl.when(p + away <= last)
        def _():
            q = p + away
            left_slot(q, c).wait_recv()

            @pl.when(p > 0)
            def _():
                left_slot(q, c).start()

    def emit(c):
        def one(t, _):
            total = jnp.zeros((rows, tile), jnp.float32)
            for q in range(planes):
                for s in range(per_plane):
                    scale = pick(q * per_plane + s, t)
                    total = total + scale * slots[q, c, :, s * tile : (s + 1) * tile].astype(jnp.float32)
            span = pl.ds(pl.multiple_of(t * tile, tile), tile)
            out_ref[pl.ds(pl.multiple_of(c * rows, rows), rows), span] = jnp.dot(
                total.astype(jnp.bfloat16), turn[t], preferred_element_type=jnp.float32
            ).astype(jnp.bfloat16)
            return 0

        lax.fori_loop(0, tiles, one, 0)

    stages = [collect]
    stages += [functools.partial(send_sums, away=away) for away in range(last - 1, 0, -1)]
    stages += [settle]
    stages += [functools.partial(pass_on, away=away) for away in range(1, planes)]
    stages += [emit]

    def event(n, _):
        @pl.when(n < events)
        def _():
            multiply(n)

        @pl.when(jnp.logical_and(n >= 1, n < events + 1))
        def _():
            add_cores(n - 1)

        @pl.when(jnp.logical_and(n >= 2, n < events + 2))
        def _():
            add_first(n - 2)

        for at, stage in enumerate(stages):
            since = n - planes - LAG - at
            c = jnp.maximum(since, 0) // planes

            @pl.when(jnp.logical_and(jnp.logical_and(since >= 0, c < parts), since % planes == 0))
            def _():
                stage(c)

        return 0

    lax.fori_loop(0, events + LAG + len(stages), event, 0)

    def drain(n, _):
        c, q = n // planes, n % planes
        core_copy(q, c).wait_send()

        @pl.when(q % 2 != x)
        def _():
            a_copy(q, c).wait_send()

        @pl.when(q // 2 != y)
        def _():
            b_copy(q, c).wait_send()

        @pl.when(jnp.logical_and(q % 2 == x, q // 2 != y))
        def _():
            a2_copy(q, c).wait_send()

        @pl.when(jnp.logical_and(q % 2 != x, q // 2 == y))
        def _():
            b2_copy(q, c).wait_send()

        @pl.when(jnp.logical_and(q <= p, p < last))
        def _():
            t_copy(tall.at[q, :, c], q, c, t_right, p + 1).wait_send()
            right_slot(q, c).wait_send()

        @pl.when(jnp.logical_and(q >= p, p > 0))
        def _():
            t_copy(tall.at[q, :, c], q, c, t_left, p - 1).wait_send()
            left_slot(q, c).wait_send()

        @pl.when(q > p)
        def _():
            right_sum(q, c).wait_send()

        @pl.when(q < p)
        def _():
            left_sum(q, c).wait_send()

        return 0

    lax.fori_loop(0, events, drain, 0)


def shards(planes, amplitudes, integrals, sym_rows, sym_cols, mirror_rows):
    tiles = sym_rows.shape[0]
    columns, depth = integrals.shape
    tile = columns // tiles
    all_tiles = mirror_rows.shape[0] // tile
    per_plane = all_tiles // 2 // planes
    rows = amplitudes.shape[0] // (CORES * PARTS)

    dma = pltpu.SemaphoreType.DMA
    grid = (planes, PARTS)
    vmem = pl.BlockSpec(memory_space=pltpu.VMEM)
    smem = pl.BlockSpec(memory_space=pltpu.SMEM)
    hbm = pl.BlockSpec(memory_space=pl.ANY)
    group = per_plane * tile
    return pl.pallas_call(
        functools.partial(ladder_kernel, planes, tiles, tile),
        out_shape=jax.ShapeDtypeStruct((PARTS * rows, columns), jnp.bfloat16),
        in_specs=[hbm, hbm, smem, smem, smem, vmem],
        out_specs=vmem,
        scratch_shapes=[
            pltpu.SMEM((tiles,), jnp.int32),
            pltpu.VMEM((tiles, tile, tile), jnp.bfloat16),
            pltpu.VMEM((columns, depth), jnp.bfloat16),
            pltpu.VMEM((depth, columns), jnp.bfloat16),
            pltpu.VMEM((planes, CORES, PARTS, rows, depth), jnp.bfloat16),
            pltpu.VMEM((planes, CORES, PARTS, rows, columns), jnp.float32),
            pltpu.VMEM((planes, PARTS, rows, columns), jnp.float32),
            pltpu.VMEM((planes, PARTS, rows, columns), jnp.float32),
            pltpu.VMEM((PARTS, rows, columns), jnp.float32),
            pltpu.VMEM((planes, PARTS, rows, group), jnp.float32),
            pltpu.VMEM((planes, PARTS, rows, group), jnp.float32),
            pltpu.VMEM((planes, PARTS, rows, group), jnp.float32),
            pltpu.VMEM((planes, PARTS, rows, group), jnp.bfloat16),
            dma, dma,
            dma(grid), dma(grid), dma(grid), dma(grid), dma(grid),
            dma(grid), dma(grid), dma(grid), dma(grid),
            dma((PARTS,)), dma((PARTS,)), dma((PARTS,)), dma((PARTS,)),
            dma(grid), dma(grid), dma(grid), dma(grid),
            dma(grid), dma(grid), dma(grid),
        ],
        compiler_params=pltpu.CompilerParams(
            collective_id=0, has_side_effects=True, vmem_limit_bytes=48 * 1024 * 1024
        ),
        cost_estimate=pl.CostEstimate(
            flops=2 * planes * amplitudes.shape[0] * columns * depth,
            bytes_accessed=2 * (amplitudes.size + integrals.size), transcendentals=0,
        ),
    )(amplitudes.reshape(CORES, PARTS, rows, depth), integrals, sym_rows, sym_cols,
      mirror_rows, mirror_rows.reshape(all_tiles, tile))


def solution(mesh):
    planes, chips = mesh.shape["pair"], mesh.shape["intg"] // CORES
    direct = planes == chips and chips == SIDE * SIDE
    body = functools.partial(shards, planes) if direct else shards_plain
    return jax.shard_map(
        body,
        mesh=mesh,
        in_specs=(P("pair", "intg"), P("pair", "intg"), P("pair"), P("intg"), P()),
        out_specs=P("intg", "pair"),
        check_vma=False,
    )
```

```python
import functools

import jax
import jax.numpy as jnp
from jax import lax
from jax.experimental import pallas as pl
from jax.experimental.pallas import tpu as pltpu
from jax.sharding import PartitionSpec as P

MESH = pl.DeviceIdType.MESH
PARTS = 4
LAG = 4
SPACE = 2
AHEAD = 2
CORES = 2
SIDE = 2


def contract_pair(left, right):
    return lax.dot_general(
        left, right, (((1,), (1,)), ((), ())), preferred_element_type=jnp.float32
    )


def shards_plain(amplitudes, integrals, sym_rows, sym_cols, mirror_rows):
    tile_rows = integrals.shape[0] // sym_rows.shape[0]
    row_sym = jnp.repeat(sym_rows, tile_rows)
    col_sym = jnp.repeat(sym_cols, tile_rows)
    masked = jnp.where(row_sym[:, None] == col_sym[None, :], integrals, jnp.zeros((), jnp.bfloat16))
    ab_rows = integrals.shape[0]
    own_twins = lax.dynamic_slice_in_dim(mirror_rows, lax.axis_index("pair") * ab_rows, ab_rows, 0)
    partial_sums = contract_pair(lax.all_gather(amplitudes, "pair", axis=0, tiled=True), masked)
    result_block = lax.psum_scatter(partial_sums, "intg", scatter_dimension=0, tiled=True)
    all_columns = lax.all_gather(result_block, "pair", axis=1, tiled=True)
    result_block = result_block - jnp.take(all_columns, own_twins, axis=1)
    return result_block.astype(jnp.bfloat16)


def ladder_kernel(
    planes, tiles, tile,
    t_ref, v_ref, rows_ref, cols_ref, mirror_ref, twin_ref, out_ref,
    rank_ref, turn, v_in, turned, tall, prod, from_core, hop_one, hop_two, cont, from_left, from_right, slots,
    v_sem, own_sem, t_recv, t_right, t_left, core_send, core_recv,
    a_send, a_recv, b_send, b_recv, a2_send, a2_recv, b2_send, b2_recv,
    zr_send, zr_recv, zl_send, zl_recv, gr_send, gl_send, g_recv,
):
    parts, rows, depth = t_ref.shape[1], t_ref.shape[2], t_ref.shape[3]
    columns = prod.shape[-1]
    half = columns // 2
    group = cont.shape[-1]
    per_plane = group // tile
    last = planes - 1
    p = lax.axis_index("pair")
    g = lax.axis_index("intg")
    core, x, y = g % 2, (g // 2) % 2, g // 4
    chip = g // 2
    sibling = g + 1 - 2 * core
    x_peer = g + 2 - 4 * x
    y_peer = g + 4 - 8 * y
    low, high = slice(0, half), slice(half, columns)

    def order(step):
        result = jnp.int32(0)
        for plane in range(planes):
            near = sorted(range(planes), key=lambda q: abs(q - plane))
            for at, q in enumerate(near):
                result = result + jnp.where(jnp.logical_and(p == plane, step == at), q, 0)
        return result

    load_v = pltpu.make_async_copy(v_ref, v_in, v_sem)
    load_v.start()
    load_t = pltpu.make_async_copy(t_ref, tall.at[p], own_sem)
    load_t.start()

    barrier = pltpu.get_barrier_semaphore()
    for peer in (sibling, x_peer, y_peer):
        pl.semaphore_signal(barrier, inc=1, device_id={"intg": peer}, device_id_type=MESH)

    @pl.when(p > 0)
    def _():
        pl.semaphore_signal(barrier, inc=1, device_id={"pair": p - 1}, device_id_type=MESH)

    @pl.when(p < last)
    def _():
        pl.semaphore_signal(barrier, inc=1, device_id={"pair": p + 1}, device_id_type=MESH)

    ends = (p == 0).astype(jnp.int32) + (p == last).astype(jnp.int32)
    pl.semaphore_wait(barrier, 5 - ends)

    def remote(src, dst, send, recv, **where):
        return pltpu.make_async_remote_copy(
            src_ref=src, dst_ref=dst, send_sem=send, recv_sem=recv,
            device_id=where, device_id_type=MESH,
        )

    def t_copy(src, q, c, send, plane):
        return remote(src, tall.at[q, :, c], send.at[q, c], t_recv.at[q, c], pair=plane)

    def own_t(c):
        @pl.when(p < last)
        def _():
            t_copy(t_ref.at[:, c], p, c, t_right, p + 1).start()

        @pl.when(p > 0)
        def _():
            t_copy(t_ref.at[:, c], p, c, t_left, p - 1).start()

    for c in range(AHEAD):
        own_t(c)

    all_tiles = planes * tiles
    base = p * tiles
    partners = [mirror_ref[u * tile] // tile for u in range(all_tiles)]
    load_v.wait()

    def prepare(t, _):
        at = base + t
        partner = mirror_ref[at * tile] // tile
        leads = at < partner
        first = jnp.minimum(at, partner)
        rank = jnp.int32(0)
        for u in range(all_tiles):
            rank = rank + jnp.where(jnp.logical_and(u < partners[u], u < first), 1, 0)
        rank_ref[t] = rank
        lane = lax.broadcasted_iota(jnp.int32, (1, tile), 1)
        spot = jnp.where(leads, lane, twin_ref[pl.ds(at, 1), :] - partner * tile)
        sign = jnp.where(leads, 1.0, -1.0)
        row = lax.broadcasted_iota(jnp.int32, (tile, tile), 0)
        turn[t] = jnp.where(row == spot, sign, 0.0).astype(jnp.bfloat16)
        span = pl.ds(pl.multiple_of(t * tile, tile), tile)
        for u in range(depth // tile):
            keep = jnp.where(rows_ref[t] == cols_ref[u], 1.0, 0.0)
            lanes = slice(u * tile, (u + 1) * tile)
            v_in[span, lanes] = (v_in[span, lanes].astype(jnp.float32) * keep).astype(jnp.bfloat16)
        turned[:, span] = jnp.dot(
            turn[t], v_in[span, :], preferred_element_type=jnp.float32
        ).T.astype(jnp.bfloat16)
        return 0

    lax.fori_loop(0, tiles, prepare, 0)
    load_t.wait()

    def core_copy(q, c):
        return remote(
            prod.at[q, 1 - core, c], from_core.at[q, c],
            core_send.at[q, c], core_recv.at[q, c], intg=sibling,
        )

    def a_copy(q, c):
        return remote(prod.at[q, core, c, :, low], hop_one.at[q, c, :, low],
                      a_send.at[q, c], a_recv.at[q, c], intg=x_peer)

    def b_copy(q, c):
        return remote(prod.at[q, core, c, :, high], hop_one.at[q, c, :, high],
                      b_send.at[q, c], b_recv.at[q, c], intg=y_peer)

    def a2_copy(q, c):
        return remote(prod.at[q, core, c, :, low], hop_two.at[c, :, low],
                      a2_send.at[c], a2_recv.at[c], intg=y_peer)

    def b2_copy(q, c):
        return remote(prod.at[q, core, c, :, high], hop_two.at[c, :, high],
                      b2_send.at[c], b2_recv.at[c], intg=x_peer)

    events = planes * parts

    def multiply(n):
        c, at = n // planes, n % planes
        q = order(at)

        @pl.when(at > 0)
        def _():
            t_copy(t_ref.at[:, c], q, c, t_right, p).wait_recv()

            @pl.when(jnp.logical_and(q < p, p < last))
            def _():
                t_copy(tall.at[q, :, c], q, c, t_right, p + 1).start()

            @pl.when(jnp.logical_and(q > p, p > 0))
            def _():
                t_copy(tall.at[q, :, c], q, c, t_left, p - 1).start()

        @pl.when(jnp.logical_and(at == 1, c + AHEAD < parts))
        def _():
            own_t(c + AHEAD)

        left = tall[q, :, c].reshape(CORES * rows, depth)
        wide = min(256, columns)

        def block(i, _):
            span = pl.ds(pl.multiple_of(i * wide, wide), wide)
            prod[q, :, c, :, span] = jnp.dot(
                left, turned[:, span], preferred_element_type=jnp.float32
            ).reshape(CORES, rows, wide)
            return 0

        lax.fori_loop(0, columns // wide, block, 0)
        core_copy(q, c).start()

    def add_cores(n):
        c, q = n // planes, order(n % planes)
        core_copy(q, c).wait_recv()
        prod[q, core, c] = prod[q, core, c] + from_core[q, c]

        @pl.when(q % 2 != x)
        def _():
            a_copy(q, c).start()

        @pl.when(q // 2 != y)
        def _():
            b_copy(q, c).start()

    def add_first(n):
        c, q = n // planes, order(n % planes)

        @pl.when(q % 2 == x)
        def _():
            a_copy(q, c).wait_recv()
            prod[q, core, c, :, low] = prod[q, core, c, :, low] + hop_one[q, c, :, low]

            @pl.when(q // 2 != y)
            def _():
                a2_copy(q, c).start()

        @pl.when(q // 2 == y)
        def _():
            b_copy(q, c).wait_recv()
            prod[q, core, c, :, high] = prod[q, core, c, :, high] + hop_one[q, c, :, high]

            @pl.when(q % 2 != x)
            def _():
                b2_copy(q, c).start()

    def right_sum(q, c):
        return remote(cont.at[q, c], from_left.at[q, c], zr_send.at[q, c], zr_recv.at[q, c], pair=p + 1)

    def left_sum(q, c):
        return remote(cont.at[q, c], from_right.at[q, c], zl_send.at[q, c], zl_recv.at[q, c], pair=p - 1)

    def pick(k, t):
        return jnp.where(rank_ref[t] == k, 1.0, 0.0)

    def collect(c):
        a2_copy(chip, c).wait_recv()
        b2_copy(chip, c).wait_recv()
        prod[chip, core, c] = prod[chip, core, c] + hop_two[c]

        def fill(k, _):
            total = jnp.zeros((rows, tile), jnp.float32)
            for t in range(tiles):
                total = total + pick(k, t) * prod[chip, core, c, :, t * tile : (t + 1) * tile]
            span = pl.ds(pl.multiple_of(k % per_plane * tile, tile), tile)
            cont[k // per_plane, c, :, span] = total
            return 0

        lax.fori_loop(0, planes * per_plane, fill, 0)
        send_sums(c, last)

    def send_sums(c, away):
        @pl.when(p + away <= last)
        def _():
            q = p + away

            @pl.when(p > 0)
            def _():
                right_sum(q, c).wait_recv()
                cont[q, c] = cont[q, c] + from_left[q, c]

            right_sum(q, c).start()

        @pl.when(p - away >= 0)
        def _():
            q = p - away

            @pl.when(p < last)
            def _():
                left_sum(q, c).wait_recv()
                cont[q, c] = cont[q, c] + from_right[q, c]

            left_sum(q, c).start()

    def right_slot(q, c):
        return remote(slots.at[q, c], slots.at[q, c], gr_send.at[q, c], g_recv.at[q, c], pair=p + 1)

    def left_slot(q, c):
        return remote(slots.at[q, c], slots.at[q, c], gl_send.at[q, c], g_recv.at[q, c], pair=p - 1)

    def settle(c):
        @pl.when(p > 0)
        def _():
            right_sum(p, c).wait_recv()
            cont[p, c] = cont[p, c] + from_left[p, c]

        @pl.when(p < last)
        def _():
            left_sum(p, c).wait_recv()
            cont[p, c] = cont[p, c] + from_right[p, c]

        slots[p, c] = cont[p, c].astype(jnp.bfloat16)

        @pl.when(p < last)
        def _():
            right_slot(p, c).start()

        @pl.when(p > 0)
        def _():
            left_slot(p, c).start()

    def pass_on(c, away):
        @pl.when(p - away >= 0)
        def _():
            q = p - away
            right_slot(q, c).wait_recv()

            @pl.when(p < last)
            def _():
                right_slot(q, c).start()

        @pl.when(p + away <= last)
        def _():
            q = p + away
            left_slot(q, c).wait_recv()

            @pl.when(p > 0)
            def _():
                left_slot(q, c).start()

    def emit(c):
        def one(t, _):
            total = jnp.zeros((rows, tile), jnp.float32)
            for q in range(planes):
                for s in range(per_plane):
                    scale = pick(q * per_plane + s, t)
                    total = total + scale * slots[q, c, :, s * tile : (s + 1) * tile].astype(jnp.float32)
            span = pl.ds(pl.multiple_of(t * tile, tile), tile)
            out_ref[pl.ds(pl.multiple_of(c * rows, rows), rows), span] = jnp.dot(
                total.astype(jnp.bfloat16), turn[t], preferred_element_type=jnp.float32
            ).astype(jnp.bfloat16)
            return 0

        lax.fori_loop(0, tiles, one, 0)

    stages = [collect]
    stages += [functools.partial(send_sums, away=away) for away in range(last - 1, 0, -1)]
    stages += [settle]
    stages += [functools.partial(pass_on, away=away) for away in range(1, planes)]
    stages += [emit]

    def event(n, _):
        @pl.when(n < events)
        def _():
            multiply(n)

        @pl.when(jnp.logical_and(n >= 1, n < events + 1))
        def _():
            add_cores(n - 1)

        @pl.when(jnp.logical_and(n >= 1 + SPACE, n < events + 1 + SPACE))
        def _():
            add_first(n - 1 - SPACE)

        for at, stage in enumerate(stages):
            since = n - planes - LAG - at * SPACE
            c = jnp.maximum(since, 0) // planes

            @pl.when(jnp.logical_and(jnp.logical_and(since >= 0, c < parts), since % planes == 0))
            def _():
                stage(c)

        return 0

    lax.fori_loop(0, events + LAG + SPACE * len(stages), event, 0)

    def drain(n, _):
        c, q = n // planes, n % planes
        core_copy(q, c).wait_send()

        @pl.when(q % 2 != x)
        def _():
            a_copy(q, c).wait_send()

        @pl.when(q // 2 != y)
        def _():
            b_copy(q, c).wait_send()

        @pl.when(jnp.logical_and(q % 2 == x, q // 2 != y))
        def _():
            a2_copy(q, c).wait_send()

        @pl.when(jnp.logical_and(q % 2 != x, q // 2 == y))
        def _():
            b2_copy(q, c).wait_send()

        @pl.when(jnp.logical_and(q <= p, p < last))
        def _():
            t_copy(tall.at[q, :, c], q, c, t_right, p + 1).wait_send()
            right_slot(q, c).wait_send()

        @pl.when(jnp.logical_and(q >= p, p > 0))
        def _():
            t_copy(tall.at[q, :, c], q, c, t_left, p - 1).wait_send()
            left_slot(q, c).wait_send()

        @pl.when(q > p)
        def _():
            right_sum(q, c).wait_send()

        @pl.when(q < p)
        def _():
            left_sum(q, c).wait_send()

        return 0

    lax.fori_loop(0, events, drain, 0)


def shards(planes, amplitudes, integrals, sym_rows, sym_cols, mirror_rows):
    tiles = sym_rows.shape[0]
    columns, depth = integrals.shape
    tile = columns // tiles
    all_tiles = mirror_rows.shape[0] // tile
    per_plane = all_tiles // 2 // planes
    rows = amplitudes.shape[0] // (CORES * PARTS)

    dma = pltpu.SemaphoreType.DMA
    grid = (planes, PARTS)
    vmem = pl.BlockSpec(memory_space=pltpu.VMEM)
    smem = pl.BlockSpec(memory_space=pltpu.SMEM)
    hbm = pl.BlockSpec(memory_space=pl.ANY)
    group = per_plane * tile
    return pl.pallas_call(
        functools.partial(ladder_kernel, planes, tiles, tile),
        out_shape=jax.ShapeDtypeStruct((PARTS * rows, columns), jnp.bfloat16),
        in_specs=[hbm, hbm, smem, smem, smem, vmem],
        out_specs=vmem,
        scratch_shapes=[
            pltpu.SMEM((tiles,), jnp.int32),
            pltpu.VMEM((tiles, tile, tile), jnp.bfloat16),
            pltpu.VMEM((columns, depth), jnp.bfloat16),
            pltpu.VMEM((depth, columns), jnp.bfloat16),
            pltpu.VMEM((planes, CORES, PARTS, rows, depth), jnp.bfloat16),
            pltpu.VMEM((planes, CORES, PARTS, rows, columns), jnp.float32),
            pltpu.VMEM((planes, PARTS, rows, columns), jnp.float32),
            pltpu.VMEM((planes, PARTS, rows, columns), jnp.float32),
            pltpu.VMEM((PARTS, rows, columns), jnp.float32),
            pltpu.VMEM((planes, PARTS, rows, group), jnp.float32),
            pltpu.VMEM((planes, PARTS, rows, group), jnp.float32),
            pltpu.VMEM((planes, PARTS, rows, group), jnp.float32),
            pltpu.VMEM((planes, PARTS, rows, group), jnp.bfloat16),
            dma, dma,
            dma(grid), dma(grid), dma(grid), dma(grid), dma(grid),
            dma(grid), dma(grid), dma(grid), dma(grid),
            dma((PARTS,)), dma((PARTS,)), dma((PARTS,)), dma((PARTS,)),
            dma(grid), dma(grid), dma(grid), dma(grid),
            dma(grid), dma(grid), dma(grid),
        ],
        compiler_params=pltpu.CompilerParams(
            collective_id=0, has_side_effects=True, vmem_limit_bytes=48 * 1024 * 1024
        ),
        cost_estimate=pl.CostEstimate(
            flops=2 * planes * amplitudes.shape[0] * columns * depth,
            bytes_accessed=2 * (amplitudes.size + integrals.size), transcendentals=0,
        ),
    )(amplitudes.reshape(CORES, PARTS, rows, depth), integrals, sym_rows, sym_cols,
      mirror_rows, mirror_rows.reshape(all_tiles, tile))


def solution(mesh):
    planes, chips = mesh.shape["pair"], mesh.shape["intg"] // CORES
    direct = planes == chips and chips == SIDE * SIDE
    body = functools.partial(shards, planes) if direct else shards_plain
    return jax.shard_map(
        body,
        mesh=mesh,
        in_specs=(P("pair", "intg"), P("pair", "intg"), P("pair"), P("intg"), P()),
        out_specs=P("intg", "pair"),
        check_vma=False,
    )
```

```python
import functools

import jax
import jax.numpy as jnp
from jax import lax
from jax.experimental import pallas as pl
from jax.experimental.pallas import tpu as pltpu
from jax.sharding import PartitionSpec as P

MESH = pl.DeviceIdType.MESH
PARTS = 4
LAG = 4
SPACE = 2
AHEAD = 2
CORES = 2
SIDE = 2


def contract_pair(left, right):
    return lax.dot_general(
        left, right, (((1,), (1,)), ((), ())), preferred_element_type=jnp.float32
    )


def shards_plain(amplitudes, integrals, sym_rows, sym_cols, mirror_rows):
    tile_rows = integrals.shape[0] // sym_rows.shape[0]
    row_sym = jnp.repeat(sym_rows, tile_rows)
    col_sym = jnp.repeat(sym_cols, tile_rows)
    masked = jnp.where(row_sym[:, None] == col_sym[None, :], integrals, jnp.zeros((), jnp.bfloat16))
    ab_rows = integrals.shape[0]
    own_twins = lax.dynamic_slice_in_dim(mirror_rows, lax.axis_index("pair") * ab_rows, ab_rows, 0)
    partial_sums = contract_pair(lax.all_gather(amplitudes, "pair", axis=0, tiled=True), masked)
    result_block = lax.psum_scatter(partial_sums, "intg", scatter_dimension=0, tiled=True)
    all_columns = lax.all_gather(result_block, "pair", axis=1, tiled=True)
    result_block = result_block - jnp.take(all_columns, own_twins, axis=1)
    return result_block.astype(jnp.bfloat16)


def ladder_kernel(
    planes, tiles, tile,
    t_ref, v_ref, rows_ref, cols_ref, mirror_ref, twin_ref, out_ref,
    rank_ref, turn, v_in, turned, tall, prod, from_core, hop_one, hop_two, cont, from_left, from_right, slots,
    v_sem, own_sem, t_recv, t_right, t_left, core_send, core_recv,
    a_send, a_recv, b_send, b_recv, a2_send, a2_recv, b2_send, b2_recv,
    zr_send, zr_recv, zl_send, zl_recv, g_send, g_recv,
):
    parts, rows, depth = t_ref.shape[1], t_ref.shape[2], t_ref.shape[3]
    columns = prod.shape[-1]
    half = columns // 2
    group = cont.shape[-1]
    per_plane = group // tile
    last = planes - 1
    p = lax.axis_index("pair")
    g = lax.axis_index("intg")
    core, x, y = g % 2, (g // 2) % 2, g // 4
    chip = g // 2
    sibling = g + 1 - 2 * core
    x_peer = g + 2 - 4 * x
    y_peer = g + 4 - 8 * y
    low, high = slice(0, half), slice(half, columns)

    def order(step):
        result = jnp.int32(0)
        for plane in range(planes):
            near = sorted(range(planes), key=lambda q: abs(q - plane))
            for at, q in enumerate(near):
                result = result + jnp.where(jnp.logical_and(p == plane, step == at), q, 0)
        return result

    load_v = pltpu.make_async_copy(v_ref, v_in, v_sem)
    load_v.start()
    load_t = pltpu.make_async_copy(t_ref, tall.at[p], own_sem)
    load_t.start()

    barrier = pltpu.get_barrier_semaphore()
    for peer in (sibling, x_peer, y_peer):
        pl.semaphore_signal(barrier, inc=1, device_id={"intg": peer}, device_id_type=MESH)

    for away in range(1, planes):
        pl.semaphore_signal(
            barrier, inc=1, device_id={"pair": (p + away) % planes}, device_id_type=MESH)
    pl.semaphore_wait(barrier, 3 + last)

    def remote(src, dst, send, recv, **where):
        return pltpu.make_async_remote_copy(
            src_ref=src, dst_ref=dst, send_sem=send, recv_sem=recv,
            device_id=where, device_id_type=MESH,
        )

    def t_copy(src, q, c, send, plane):
        return remote(src, tall.at[q, :, c], send.at[q, c], t_recv.at[q, c], pair=plane)

    def own_t(c):
        @pl.when(p < last)
        def _():
            t_copy(t_ref.at[:, c], p, c, t_right, p + 1).start()

        @pl.when(p > 0)
        def _():
            t_copy(t_ref.at[:, c], p, c, t_left, p - 1).start()

    for c in range(AHEAD):
        own_t(c)

    all_tiles = planes * tiles
    base = p * tiles
    partners = [mirror_ref[u * tile] // tile for u in range(all_tiles)]
    load_v.wait()

    def prepare(t, _):
        at = base + t
        partner = mirror_ref[at * tile] // tile
        leads = at < partner
        first = jnp.minimum(at, partner)
        rank = jnp.int32(0)
        for u in range(all_tiles):
            rank = rank + jnp.where(jnp.logical_and(u < partners[u], u < first), 1, 0)
        rank_ref[t] = rank
        lane = lax.broadcasted_iota(jnp.int32, (1, tile), 1)
        spot = jnp.where(leads, lane, twin_ref[pl.ds(at, 1), :] - partner * tile)
        sign = jnp.where(leads, 1.0, -1.0)
        row = lax.broadcasted_iota(jnp.int32, (tile, tile), 0)
        turn[t] = jnp.where(row == spot, sign, 0.0).astype(jnp.bfloat16)
        span = pl.ds(pl.multiple_of(t * tile, tile), tile)
        for u in range(depth // tile):
            keep = jnp.where(rows_ref[t] == cols_ref[u], 1.0, 0.0)
            lanes = slice(u * tile, (u + 1) * tile)
            v_in[span, lanes] = (v_in[span, lanes].astype(jnp.float32) * keep).astype(jnp.bfloat16)
        turned[:, span] = jnp.dot(
            turn[t], v_in[span, :], preferred_element_type=jnp.float32
        ).T.astype(jnp.bfloat16)
        return 0

    lax.fori_loop(0, tiles, prepare, 0)
    load_t.wait()

    def core_copy(q, c):
        return remote(
            prod.at[q, 1 - core, c], from_core.at[q, c],
            core_send.at[q, c], core_recv.at[q, c], intg=sibling,
        )

    def a_copy(q, c):
        return remote(prod.at[q, core, c, :, low], hop_one.at[q, c, :, low],
                      a_send.at[q, c], a_recv.at[q, c], intg=x_peer)

    def b_copy(q, c):
        return remote(prod.at[q, core, c, :, high], hop_one.at[q, c, :, high],
                      b_send.at[q, c], b_recv.at[q, c], intg=y_peer)

    def a2_copy(q, c):
        return remote(prod.at[q, core, c, :, low], hop_two.at[c, :, low],
                      a2_send.at[c], a2_recv.at[c], intg=y_peer)

    def b2_copy(q, c):
        return remote(prod.at[q, core, c, :, high], hop_two.at[c, :, high],
                      b2_send.at[c], b2_recv.at[c], intg=x_peer)

    events = planes * parts

    def multiply(n):
        c, at = n // planes, n % planes
        q = order(at)

        @pl.when(at > 0)
        def _():
            t_copy(t_ref.at[:, c], q, c, t_right, p).wait_recv()

            @pl.when(jnp.logical_and(q < p, p < last))
            def _():
                t_copy(tall.at[q, :, c], q, c, t_right, p + 1).start()

            @pl.when(jnp.logical_and(q > p, p > 0))
            def _():
                t_copy(tall.at[q, :, c], q, c, t_left, p - 1).start()

        @pl.when(jnp.logical_and(at == 1, c + AHEAD < parts))
        def _():
            own_t(c + AHEAD)

        left = tall[q, :, c].reshape(CORES * rows, depth)
        wide = min(256, columns)

        def block(i, _):
            span = pl.ds(pl.multiple_of(i * wide, wide), wide)
            prod[q, :, c, :, span] = jnp.dot(
                left, turned[:, span], preferred_element_type=jnp.float32
            ).reshape(CORES, rows, wide)
            return 0

        lax.fori_loop(0, columns // wide, block, 0)
        core_copy(q, c).start()

    def add_cores(n):
        c, q = n // planes, order(n % planes)
        core_copy(q, c).wait_recv()
        prod[q, core, c] = prod[q, core, c] + from_core[q, c]

        @pl.when(q % 2 != x)
        def _():
            a_copy(q, c).start()

        @pl.when(q // 2 != y)
        def _():
            b_copy(q, c).start()

    def add_first(n):
        c, q = n // planes, order(n % planes)

        @pl.when(q % 2 == x)
        def _():
            a_copy(q, c).wait_recv()
            prod[q, core, c, :, low] = prod[q, core, c, :, low] + hop_one[q, c, :, low]

            @pl.when(q // 2 != y)
            def _():
                a2_copy(q, c).start()

        @pl.when(q // 2 == y)
        def _():
            b_copy(q, c).wait_recv()
            prod[q, core, c, :, high] = prod[q, core, c, :, high] + hop_one[q, c, :, high]

            @pl.when(q % 2 != x)
            def _():
                b2_copy(q, c).start()

    def right_sum(q, c):
        return remote(cont.at[q, c], from_left.at[q, c], zr_send.at[q, c], zr_recv.at[q, c], pair=p + 1)

    def left_sum(q, c):
        return remote(cont.at[q, c], from_right.at[q, c], zl_send.at[q, c], zl_recv.at[q, c], pair=p - 1)

    def pick(k, t):
        return jnp.where(rank_ref[t] == k, 1.0, 0.0)

    def collect(c):
        a2_copy(chip, c).wait_recv()
        b2_copy(chip, c).wait_recv()
        prod[chip, core, c] = prod[chip, core, c] + hop_two[c]

        def fill(k, _):
            total = jnp.zeros((rows, tile), jnp.float32)
            for t in range(tiles):
                total = total + pick(k, t) * prod[chip, core, c, :, t * tile : (t + 1) * tile]
            span = pl.ds(pl.multiple_of(k % per_plane * tile, tile), tile)
            cont[k // per_plane, c, :, span] = total
            return 0

        lax.fori_loop(0, planes * per_plane, fill, 0)
        send_sums(c, last)

    def send_sums(c, away):
        @pl.when(p + away <= last)
        def _():
            q = p + away

            @pl.when(p > 0)
            def _():
                right_sum(q, c).wait_recv()
                cont[q, c] = cont[q, c] + from_left[q, c]

            right_sum(q, c).start()

        @pl.when(p - away >= 0)
        def _():
            q = p - away

            @pl.when(p < last)
            def _():
                left_sum(q, c).wait_recv()
                cont[q, c] = cont[q, c] + from_right[q, c]

            left_sum(q, c).start()

    def slot_copy(q, c, away, plane):
        return remote(slots.at[q, c], slots.at[q, c], g_send.at[away, c], g_recv.at[q, c], pair=plane)

    def settle(c):
        @pl.when(p > 0)
        def _():
            right_sum(p, c).wait_recv()
            cont[p, c] = cont[p, c] + from_left[p, c]

        @pl.when(p < last)
        def _():
            left_sum(p, c).wait_recv()
            cont[p, c] = cont[p, c] + from_right[p, c]

        slots[p, c] = cont[p, c].astype(jnp.bfloat16)

        for away in range(last, 0, -1):
            @pl.when(p + away <= last)
            def _():
                slot_copy(p, c, away, p + away).start()

            @pl.when(p - away >= 0)
            def _():
                slot_copy(p, c, planes - away, p - away).start()

    def emit(c):
        for q in range(planes):
            @pl.when(q != p)
            def _():
                slot_copy(q, c, 0, p).wait_recv()

        def one(t, _):
            total = jnp.zeros((rows, tile), jnp.float32)
            for q in range(planes):
                for s in range(per_plane):
                    scale = pick(q * per_plane + s, t)
                    total = total + scale * slots[q, c, :, s * tile : (s + 1) * tile].astype(jnp.float32)
            span = pl.ds(pl.multiple_of(t * tile, tile), tile)
            out_ref[pl.ds(pl.multiple_of(c * rows, rows), rows), span] = jnp.dot(
                total.astype(jnp.bfloat16), turn[t], preferred_element_type=jnp.float32
            ).astype(jnp.bfloat16)
            return 0

        lax.fori_loop(0, tiles, one, 0)

    stages = [collect]
    stages += [functools.partial(send_sums, away=away) for away in range(last - 1, 0, -1)]
    stages += [settle]
    stages += [emit]

    def event(n, _):
        @pl.when(n < events)
        def _():
            multiply(n)

        @pl.when(jnp.logical_and(n >= 1, n < events + 1))
        def _():
            add_cores(n - 1)

        @pl.when(jnp.logical_and(n >= 1 + SPACE, n < events + 1 + SPACE))
        def _():
            add_first(n - 1 - SPACE)

        for at, stage in enumerate(stages):
            since = n - planes - LAG - at * SPACE
            final = since == events - planes - LAG + SPACE
            c = jnp.where(final, parts - 1, jnp.maximum(since, 0) // planes)
            early = jnp.logical_and(jnp.logical_and(since >= 0, since % planes == 0), c < parts - 1)

            @pl.when(jnp.logical_or(final, early))
            def _():
                stage(c)

        return 0

    lax.fori_loop(0, events + 1 + SPACE * len(stages), event, 0)

    def drain(n, _):
        c, q = n // planes, n % planes
        core_copy(q, c).wait_send()

        @pl.when(q % 2 != x)
        def _():
            a_copy(q, c).wait_send()

        @pl.when(q // 2 != y)
        def _():
            b_copy(q, c).wait_send()

        @pl.when(jnp.logical_and(q % 2 == x, q // 2 != y))
        def _():
            a2_copy(q, c).wait_send()

        @pl.when(jnp.logical_and(q % 2 != x, q // 2 == y))
        def _():
            b2_copy(q, c).wait_send()

        @pl.when(jnp.logical_and(q <= p, p < last))
        def _():
            t_copy(tall.at[q, :, c], q, c, t_right, p + 1).wait_send()

        @pl.when(jnp.logical_and(q >= p, p > 0))
        def _():
            t_copy(tall.at[q, :, c], q, c, t_left, p - 1).wait_send()

        @pl.when(q > p)
        def _():
            slot_copy(p, c, q - p, q).wait_send()
            right_sum(q, c).wait_send()

        @pl.when(q < p)
        def _():
            slot_copy(p, c, planes - p + q, q).wait_send()
            left_sum(q, c).wait_send()

        return 0

    lax.fori_loop(0, events, drain, 0)


def shards(planes, amplitudes, integrals, sym_rows, sym_cols, mirror_rows):
    tiles = sym_rows.shape[0]
    columns, depth = integrals.shape
    tile = columns // tiles
    all_tiles = mirror_rows.shape[0] // tile
    per_plane = all_tiles // 2 // planes
    rows = amplitudes.shape[0] // (CORES * PARTS)

    dma = pltpu.SemaphoreType.DMA
    grid = (planes, PARTS)
    vmem = pl.BlockSpec(memory_space=pltpu.VMEM)
    smem = pl.BlockSpec(memory_space=pltpu.SMEM)
    hbm = pl.BlockSpec(memory_space=pl.ANY)
    group = per_plane * tile
    return pl.pallas_call(
        functools.partial(ladder_kernel, planes, tiles, tile),
        out_shape=jax.ShapeDtypeStruct((PARTS * rows, columns), jnp.bfloat16),
        in_specs=[hbm, hbm, smem, smem, smem, vmem],
        out_specs=vmem,
        scratch_shapes=[
            pltpu.SMEM((tiles,), jnp.int32),
            pltpu.VMEM((tiles, tile, tile), jnp.bfloat16),
            pltpu.VMEM((columns, depth), jnp.bfloat16),
            pltpu.VMEM((depth, columns), jnp.bfloat16),
            pltpu.VMEM((planes, CORES, PARTS, rows, depth), jnp.bfloat16),
            pltpu.VMEM((planes, CORES, PARTS, rows, columns), jnp.float32),
            pltpu.VMEM((planes, PARTS, rows, columns), jnp.float32),
            pltpu.VMEM((planes, PARTS, rows, columns), jnp.float32),
            pltpu.VMEM((PARTS, rows, columns), jnp.float32),
            pltpu.VMEM((planes, PARTS, rows, group), jnp.float32),
            pltpu.VMEM((planes, PARTS, rows, group), jnp.float32),
            pltpu.VMEM((planes, PARTS, rows, group), jnp.float32),
            pltpu.VMEM((planes, PARTS, rows, group), jnp.bfloat16),
            dma, dma,
            dma(grid), dma(grid), dma(grid), dma(grid), dma(grid),
            dma(grid), dma(grid), dma(grid), dma(grid),
            dma((PARTS,)), dma((PARTS,)), dma((PARTS,)), dma((PARTS,)),
            dma(grid), dma(grid), dma(grid), dma(grid),
            dma(grid), dma(grid),
        ],
        compiler_params=pltpu.CompilerParams(
            collective_id=0, has_side_effects=True, vmem_limit_bytes=60 * 1024 * 1024
        ),
        cost_estimate=pl.CostEstimate(
            flops=2 * planes * amplitudes.shape[0] * columns * depth,
            bytes_accessed=2 * (amplitudes.size + integrals.size), transcendentals=0,
        ),
    )(amplitudes.reshape(CORES, PARTS, rows, depth), integrals, sym_rows, sym_cols,
      mirror_rows, mirror_rows.reshape(all_tiles, tile))


def solution(mesh):
    planes, chips = mesh.shape["pair"], mesh.shape["intg"] // CORES
    direct = planes == chips and chips == SIDE * SIDE
    body = functools.partial(shards, planes) if direct else shards_plain
    return jax.shard_map(
        body,
        mesh=mesh,
        in_specs=(P("pair", "intg"), P("pair", "intg"), P("pair"), P("intg"), P()),
        out_specs=P("intg", "pair"),
        check_vma=False,
    )
```

```python
import functools

import jax
import jax.numpy as jnp
from jax import lax
from jax.experimental import pallas as pl
from jax.experimental.pallas import tpu as pltpu
from jax.sharding import PartitionSpec as P

MESH = pl.DeviceIdType.MESH
PARTS = 4
LAG = 4
SPACE = 2
OWNERS = 2
AHEAD = 2
CORES = 2
SIDE = 2


def contract_pair(left, right):
    return lax.dot_general(
        left, right, (((1,), (1,)), ((), ())), preferred_element_type=jnp.float32
    )


def shards_plain(amplitudes, integrals, sym_rows, sym_cols, mirror_rows):
    tile_rows = integrals.shape[0] // sym_rows.shape[0]
    row_sym = jnp.repeat(sym_rows, tile_rows)
    col_sym = jnp.repeat(sym_cols, tile_rows)
    masked = jnp.where(row_sym[:, None] == col_sym[None, :], integrals, jnp.zeros((), jnp.bfloat16))
    ab_rows = integrals.shape[0]
    own_twins = lax.dynamic_slice_in_dim(mirror_rows, lax.axis_index("pair") * ab_rows, ab_rows, 0)
    partial_sums = contract_pair(lax.all_gather(amplitudes, "pair", axis=0, tiled=True), masked)
    result_block = lax.psum_scatter(partial_sums, "intg", scatter_dimension=0, tiled=True)
    all_columns = lax.all_gather(result_block, "pair", axis=1, tiled=True)
    result_block = result_block - jnp.take(all_columns, own_twins, axis=1)
    return result_block.astype(jnp.bfloat16)


def ladder_kernel(
    planes, tiles, tile,
    t_ref, v_ref, rows_ref, cols_ref, mirror_ref, twin_ref, out_ref,
    rank_ref, turn, v_in, turned, tall, prod, from_core, hop_one, hop_two, cont, from_left, from_right, slots,
    v_sem, own_sem, t_recv, t_right, t_left, core_send, core_recv,
    a_send, a_recv, b_send, b_recv, a2_send, a2_recv, b2_send, b2_recv,
    zr_send, zr_recv, zl_send, zl_recv, g_send, g_recv,
):
    parts, rows, depth = t_ref.shape[1], t_ref.shape[2], t_ref.shape[3]
    columns = prod.shape[-1]
    half = columns // 2
    group = cont.shape[-1]
    per_owner = group // tile
    last = planes - 1
    p = lax.axis_index("pair")
    g = lax.axis_index("intg")
    core, x, y = g % 2, (g // 2) % 2, g // 4
    chip = g // 2
    sibling = g + 1 - 2 * core
    x_peer = g + 2 - 4 * x
    y_peer = g + 4 - 8 * y
    low, high = slice(0, half), slice(half, columns)

    def order(step):
        result = jnp.int32(0)
        for plane in range(planes):
            near = sorted(range(planes), key=lambda q: abs(q - plane))
            for at, q in enumerate(near):
                result = result + jnp.where(jnp.logical_and(p == plane, step == at), q, 0)
        return result

    load_v = pltpu.make_async_copy(v_ref, v_in, v_sem)
    load_v.start()
    load_t = pltpu.make_async_copy(t_ref, tall.at[p], own_sem)
    load_t.start()

    barrier = pltpu.get_barrier_semaphore()
    for peer in (sibling, x_peer, y_peer):
        pl.semaphore_signal(barrier, inc=1, device_id={"intg": peer}, device_id_type=MESH)

    for away in range(1, planes):
        pl.semaphore_signal(
            barrier, inc=1, device_id={"pair": (p + away) % planes}, device_id_type=MESH)
    pl.semaphore_wait(barrier, 3 + last)

    def remote(src, dst, send, recv, **where):
        return pltpu.make_async_remote_copy(
            src_ref=src, dst_ref=dst, send_sem=send, recv_sem=recv,
            device_id=where, device_id_type=MESH,
        )

    def t_copy(src, q, c, send, plane):
        return remote(src, tall.at[q, :, c], send.at[q, c], t_recv.at[q, c], pair=plane)

    def own_t(c):
        @pl.when(p < last)
        def _():
            t_copy(t_ref.at[:, c], p, c, t_right, p + 1).start()

        @pl.when(p > 0)
        def _():
            t_copy(t_ref.at[:, c], p, c, t_left, p - 1).start()

    for c in range(AHEAD):
        own_t(c)

    all_tiles = planes * tiles
    base = p * tiles
    partners = [mirror_ref[u * tile] // tile for u in range(all_tiles)]
    load_v.wait()

    def prepare(t, _):
        at = base + t
        partner = mirror_ref[at * tile] // tile
        leads = at < partner
        first = jnp.minimum(at, partner)
        rank = jnp.int32(0)
        for u in range(all_tiles):
            rank = rank + jnp.where(jnp.logical_and(u < partners[u], u < first), 1, 0)
        rank_ref[t] = rank
        lane = lax.broadcasted_iota(jnp.int32, (1, tile), 1)
        spot = jnp.where(leads, lane, twin_ref[pl.ds(at, 1), :] - partner * tile)
        sign = jnp.where(leads, 1.0, -1.0)
        row = lax.broadcasted_iota(jnp.int32, (tile, tile), 0)
        turn[t] = jnp.where(row == spot, sign, 0.0).astype(jnp.bfloat16)
        span = pl.ds(pl.multiple_of(t * tile, tile), tile)
        for u in range(depth // tile):
            keep = jnp.where(rows_ref[t] == cols_ref[u], 1.0, 0.0)
            lanes = slice(u * tile, (u + 1) * tile)
            v_in[span, lanes] = (v_in[span, lanes].astype(jnp.float32) * keep).astype(jnp.bfloat16)
        turned[:, span] = jnp.dot(
            turn[t], v_in[span, :], preferred_element_type=jnp.float32
        ).T.astype(jnp.bfloat16)
        return 0

    lax.fori_loop(0, tiles, prepare, 0)
    load_t.wait()

    def core_copy(q, c):
        return remote(
            prod.at[q, 1 - core, c], from_core.at[q, c],
            core_send.at[q, c], core_recv.at[q, c], intg=sibling,
        )

    def a_copy(q, c):
        return remote(prod.at[q, core, c, :, low], hop_one.at[q, c, :, low],
                      a_send.at[q, c], a_recv.at[q, c], intg=x_peer)

    def b_copy(q, c):
        return remote(prod.at[q, core, c, :, high], hop_one.at[q, c, :, high],
                      b_send.at[q, c], b_recv.at[q, c], intg=y_peer)

    def a2_copy(q, c):
        return remote(prod.at[q, core, c, :, low], hop_two.at[c, :, low],
                      a2_send.at[c], a2_recv.at[c], intg=y_peer)

    def b2_copy(q, c):
        return remote(prod.at[q, core, c, :, high], hop_two.at[c, :, high],
                      b2_send.at[c], b2_recv.at[c], intg=x_peer)

    events = planes * parts

    def multiply(n):
        c, at = n // planes, n % planes
        q = order(at)

        @pl.when(at > 0)
        def _():
            t_copy(t_ref.at[:, c], q, c, t_right, p).wait_recv()

            @pl.when(jnp.logical_and(q < p, p < last))
            def _():
                t_copy(tall.at[q, :, c], q, c, t_right, p + 1).start()

            @pl.when(jnp.logical_and(q > p, p > 0))
            def _():
                t_copy(tall.at[q, :, c], q, c, t_left, p - 1).start()

        @pl.when(jnp.logical_and(at == 1, c + AHEAD < parts))
        def _():
            own_t(c + AHEAD)

        left = tall[q, :, c].reshape(CORES * rows, depth)
        wide = min(256, columns)

        def block(i, _):
            span = pl.ds(pl.multiple_of(i * wide, wide), wide)
            prod[q, :, c, :, span] = jnp.dot(
                left, turned[:, span], preferred_element_type=jnp.float32
            ).reshape(CORES, rows, wide)
            return 0

        lax.fori_loop(0, columns // wide, block, 0)
        core_copy(q, c).start()

    def add_cores(n):
        c, q = n // planes, order(n % planes)
        core_copy(q, c).wait_recv()
        prod[q, core, c] = prod[q, core, c] + from_core[q, c]

        @pl.when(q % 2 != x)
        def _():
            a_copy(q, c).start()

        @pl.when(q // 2 != y)
        def _():
            b_copy(q, c).start()

    def add_first(n):
        c, q = n // planes, order(n % planes)

        @pl.when(q % 2 == x)
        def _():
            a_copy(q, c).wait_recv()
            prod[q, core, c, :, low] = prod[q, core, c, :, low] + hop_one[q, c, :, low]

            @pl.when(q // 2 != y)
            def _():
                a2_copy(q, c).start()

        @pl.when(q // 2 == y)
        def _():
            b_copy(q, c).wait_recv()
            prod[q, core, c, :, high] = prod[q, core, c, :, high] + hop_one[q, c, :, high]

            @pl.when(q % 2 != x)
            def _():
                b2_copy(q, c).start()

    def right_sum(q, c):
        return remote(cont.at[q, c], from_left.at[q, c], zr_send.at[q, c], zr_recv.at[q, c], pair=p + 1)

    def left_sum(q, c):
        return remote(cont.at[q, c], from_right.at[q, c], zl_send.at[q, c], zl_recv.at[q, c], pair=p - 1)

    def pick(k, t):
        return jnp.where(rank_ref[t] == k, 1.0, 0.0)

    def collect(c):
        a2_copy(chip, c).wait_recv()
        b2_copy(chip, c).wait_recv()
        prod[chip, core, c] = prod[chip, core, c] + hop_two[c]

        def fill(k, _):
            total = jnp.zeros((rows, tile), jnp.float32)
            for t in range(tiles):
                total = total + pick(k, t) * prod[chip, core, c, :, t * tile : (t + 1) * tile]
            span = pl.ds(pl.multiple_of(k % per_owner * tile, tile), tile)
            cont[k // per_owner, c, :, span] = total
            return 0

        lax.fori_loop(0, OWNERS * per_owner, fill, 0)

        @pl.when(p == 0)
        def _():
            right_sum(1, c).start()
            right_sum(0, c).start()

        @pl.when(p == last)
        def _():
            left_sum(0, c).start()
            left_sum(1, c).start()

    def send_on(c):
        @pl.when(p == 1)
        def _():
            right_sum(1, c).wait_recv()
            cont[1, c] = cont[1, c] + from_left[1, c]
            right_sum(1, c).start()

        @pl.when(p == 2)
        def _():
            left_sum(0, c).wait_recv()
            cont[0, c] = cont[0, c] + from_right[0, c]
            left_sum(0, c).start()

    def slot_copy(q, c, away, plane):
        return remote(slots.at[q, c], slots.at[q, c], g_send.at[away, c], g_recv.at[q, c], pair=plane)

    inner = jnp.logical_and(p > 0, p < last)
    own = jnp.clip(p - 1, 0, OWNERS - 1)

    def settle(c):
        @pl.when(inner)
        def _():
            right_sum(own, c).wait_recv()
            left_sum(own, c).wait_recv()
            slots[own, c] = (cont[own, c] + from_left[own, c] + from_right[own, c]).astype(jnp.bfloat16)
            for away in range(1, planes):
                slot_copy(own, c, away, (p + away) % planes).start()

    def emit(c):
        for q in range(OWNERS):
            @pl.when(p != q + 1)
            def _():
                slot_copy(q, c, 0, p).wait_recv()

        def one(t, _):
            total = jnp.zeros((rows, tile), jnp.float32)
            for q in range(OWNERS):
                for s in range(per_owner):
                    scale = pick(q * per_owner + s, t)
                    total = total + scale * slots[q, c, :, s * tile : (s + 1) * tile].astype(jnp.float32)
            span = pl.ds(pl.multiple_of(t * tile, tile), tile)
            out_ref[pl.ds(pl.multiple_of(c * rows, rows), rows), span] = jnp.dot(
                total.astype(jnp.bfloat16), turn[t], preferred_element_type=jnp.float32
            ).astype(jnp.bfloat16)
            return 0

        lax.fori_loop(0, tiles, one, 0)

    stages = [collect, send_on, settle, emit]

    def event(n, _):
        @pl.when(n < events)
        def _():
            multiply(n)

        @pl.when(jnp.logical_and(n >= 1, n < events + 1))
        def _():
            add_cores(n - 1)

        @pl.when(jnp.logical_and(n >= 1 + SPACE, n < events + 1 + SPACE))
        def _():
            add_first(n - 1 - SPACE)

        for at, stage in enumerate(stages):
            since = n - planes - LAG - at * SPACE
            final = since == events - planes - LAG + SPACE
            c = jnp.where(final, parts - 1, jnp.maximum(since, 0) // planes)
            early = jnp.logical_and(jnp.logical_and(since >= 0, since % planes == 0), c < parts - 1)

            @pl.when(jnp.logical_or(final, early))
            def _():
                stage(c)

        return 0

    lax.fori_loop(0, events + 1 + SPACE * len(stages), event, 0)

    def drain(n, _):
        c, q = n // planes, n % planes
        core_copy(q, c).wait_send()

        @pl.when(q % 2 != x)
        def _():
            a_copy(q, c).wait_send()

        @pl.when(q // 2 != y)
        def _():
            b_copy(q, c).wait_send()

        @pl.when(jnp.logical_and(q % 2 == x, q // 2 != y))
        def _():
            a2_copy(q, c).wait_send()

        @pl.when(jnp.logical_and(q % 2 != x, q // 2 == y))
        def _():
            b2_copy(q, c).wait_send()

        @pl.when(jnp.logical_and(q <= p, p < last))
        def _():
            t_copy(tall.at[q, :, c], q, c, t_right, p + 1).wait_send()

        @pl.when(jnp.logical_and(q >= p, p > 0))
        def _():
            t_copy(tall.at[q, :, c], q, c, t_left, p - 1).wait_send()

        @pl.when(jnp.logical_and(q < OWNERS, p == 0))
        def _():
            right_sum(q, c).wait_send()

        @pl.when(jnp.logical_and(q < OWNERS, p == last))
        def _():
            left_sum(q, c).wait_send()

        @pl.when(jnp.logical_and(q == 1, p == 1))
        def _():
            right_sum(q, c).wait_send()

        @pl.when(jnp.logical_and(q == 0, p == 2))
        def _():
            left_sum(q, c).wait_send()

        @pl.when(jnp.logical_and(inner, q > 0))
        def _():
            slot_copy(own, c, q, p).wait_send()

        return 0

    lax.fori_loop(0, events, drain, 0)


def shards(planes, amplitudes, integrals, sym_rows, sym_cols, mirror_rows):
    tiles = sym_rows.shape[0]
    columns, depth = integrals.shape
    tile = columns // tiles
    all_tiles = mirror_rows.shape[0] // tile
    per_owner = all_tiles // 2 // OWNERS
    rows = amplitudes.shape[0] // (CORES * PARTS)

    dma = pltpu.SemaphoreType.DMA
    grid = (planes, PARTS)
    vmem = pl.BlockSpec(memory_space=pltpu.VMEM)
    smem = pl.BlockSpec(memory_space=pltpu.SMEM)
    hbm = pl.BlockSpec(memory_space=pl.ANY)
    group = per_owner * tile
    return pl.pallas_call(
        functools.partial(ladder_kernel, planes, tiles, tile),
        out_shape=jax.ShapeDtypeStruct((PARTS * rows, columns), jnp.bfloat16),
        in_specs=[hbm, hbm, smem, smem, smem, vmem],
        out_specs=vmem,
        scratch_shapes=[
            pltpu.SMEM((tiles,), jnp.int32),
            pltpu.VMEM((tiles, tile, tile), jnp.bfloat16),
            pltpu.VMEM((columns, depth), jnp.bfloat16),
            pltpu.VMEM((depth, columns), jnp.bfloat16),
            pltpu.VMEM((planes, CORES, PARTS, rows, depth), jnp.bfloat16),
            pltpu.VMEM((planes, CORES, PARTS, rows, columns), jnp.float32),
            pltpu.VMEM((planes, PARTS, rows, columns), jnp.float32),
            pltpu.VMEM((planes, PARTS, rows, columns), jnp.float32),
            pltpu.VMEM((PARTS, rows, columns), jnp.float32),
            pltpu.VMEM((OWNERS, PARTS, rows, group), jnp.float32),
            pltpu.VMEM((OWNERS, PARTS, rows, group), jnp.float32),
            pltpu.VMEM((OWNERS, PARTS, rows, group), jnp.float32),
            pltpu.VMEM((OWNERS, PARTS, rows, group), jnp.bfloat16),
            dma, dma,
            dma(grid), dma(grid), dma(grid), dma(grid), dma(grid),
            dma(grid), dma(grid), dma(grid), dma(grid),
            dma((PARTS,)), dma((PARTS,)), dma((PARTS,)), dma((PARTS,)),
            dma(grid), dma(grid), dma(grid), dma(grid),
            dma(grid), dma(grid),
        ],
        compiler_params=pltpu.CompilerParams(
            collective_id=0, has_side_effects=True, vmem_limit_bytes=60 * 1024 * 1024
        ),
        cost_estimate=pl.CostEstimate(
            flops=2 * planes * amplitudes.shape[0] * columns * depth,
            bytes_accessed=2 * (amplitudes.size + integrals.size), transcendentals=0,
        ),
    )(amplitudes.reshape(CORES, PARTS, rows, depth), integrals, sym_rows, sym_cols,
      mirror_rows, mirror_rows.reshape(all_tiles, tile))


def solution(mesh):
    planes, chips = mesh.shape["pair"], mesh.shape["intg"] // CORES
    direct = planes == chips and chips == SIDE * SIDE
    body = functools.partial(shards, planes) if direct else shards_plain
    return jax.shard_map(
        body,
        mesh=mesh,
        in_specs=(P("pair", "intg"), P("pair", "intg"), P("pair"), P("intg"), P()),
        out_specs=P("intg", "pair"),
        check_vma=False,
    )
```

```python
import functools

import jax
import jax.numpy as jnp
from jax import lax
from jax.experimental import pallas as pl
from jax.experimental.pallas import tpu as pltpu
from jax.sharding import PartitionSpec as P

MESH = pl.DeviceIdType.MESH
PARTS = 4
LAG = 4
SPACE = 2
OWNERS = 2
AHEAD = 2
CORES = 2
SIDE = 2


def contract_pair(left, right):
    return lax.dot_general(
        left, right, (((1,), (1,)), ((), ())), preferred_element_type=jnp.float32
    )


def shards_plain(amplitudes, integrals, sym_rows, sym_cols, mirror_rows):
    tile_rows = integrals.shape[0] // sym_rows.shape[0]
    row_sym = jnp.repeat(sym_rows, tile_rows)
    col_sym = jnp.repeat(sym_cols, tile_rows)
    masked = jnp.where(row_sym[:, None] == col_sym[None, :], integrals, jnp.zeros((), jnp.bfloat16))
    ab_rows = integrals.shape[0]
    own_twins = lax.dynamic_slice_in_dim(mirror_rows, lax.axis_index("pair") * ab_rows, ab_rows, 0)
    partial_sums = contract_pair(lax.all_gather(amplitudes, "pair", axis=0, tiled=True), masked)
    result_block = lax.psum_scatter(partial_sums, "intg", scatter_dimension=0, tiled=True)
    all_columns = lax.all_gather(result_block, "pair", axis=1, tiled=True)
    result_block = result_block - jnp.take(all_columns, own_twins, axis=1)
    return result_block.astype(jnp.bfloat16)


def ladder_kernel(
    planes, tiles, tile,
    t_ref, v_ref, rows_ref, cols_ref, mirror_ref, twin_ref, out_ref,
    rank_ref, turn, v_in, turned, tall, prod, from_core, hop_one, hop_two, cont, from_left, from_right, slots, packs, landed,
    v_sem, own_sem, t_recv, t_right, t_left, core_send, core_recv,
    a_send, a_recv, b_send, b_recv, a2_send, a2_recv, b2_send, b2_recv,
    zr_send, zr_recv, zl_send, zl_recv, pack_send, land_recv,
):
    parts, rows, depth = t_ref.shape[1], t_ref.shape[2], t_ref.shape[3]
    columns = prod.shape[-1]
    half = columns // 2
    group = cont.shape[-1]
    per_owner = group // tile
    last = planes - 1
    p = lax.axis_index("pair")
    g = lax.axis_index("intg")
    core, x, y = g % 2, (g // 2) % 2, g // 4
    chip = g // 2
    sibling = g + 1 - 2 * core
    x_peer = g + 2 - 4 * x
    y_peer = g + 4 - 8 * y
    low, high = slice(0, half), slice(half, columns)

    def order(step):
        result = jnp.int32(0)
        for plane in range(planes):
            near = sorted(range(planes), key=lambda q: abs(q - plane))
            for at, q in enumerate(near):
                result = result + jnp.where(jnp.logical_and(p == plane, step == at), q, 0)
        return result

    load_v = pltpu.make_async_copy(v_ref, v_in, v_sem)
    load_v.start()
    load_t = pltpu.make_async_copy(t_ref, tall.at[p], own_sem)
    load_t.start()

    barrier = pltpu.get_barrier_semaphore()
    for peer in (sibling, x_peer, y_peer):
        pl.semaphore_signal(barrier, inc=1, device_id={"intg": peer}, device_id_type=MESH)

    for away in range(1, planes):
        pl.semaphore_signal(
            barrier, inc=1, device_id={"pair": (p + away) % planes}, device_id_type=MESH)
    pl.semaphore_wait(barrier, 3 + last)

    def remote(src, dst, send, recv, **where):
        return pltpu.make_async_remote_copy(
            src_ref=src, dst_ref=dst, send_sem=send, recv_sem=recv,
            device_id=where, device_id_type=MESH,
        )

    def t_copy(src, q, c, send, plane):
        return remote(src, tall.at[q, :, c], send.at[q, c], t_recv.at[q, c], pair=plane)

    def own_t(c):
        @pl.when(p < last)
        def _():
            t_copy(t_ref.at[:, c], p, c, t_right, p + 1).start()

        @pl.when(p > 0)
        def _():
            t_copy(t_ref.at[:, c], p, c, t_left, p - 1).start()

    for c in range(AHEAD):
        own_t(c)

    all_tiles = planes * tiles
    base = p * tiles
    load_v.wait()

    def prepare(t, _):
        at = base + t
        partner = mirror_ref[at * tile] // tile
        leads = at < partner
        lane = lax.broadcasted_iota(jnp.int32, (1, tile), 1)
        spot = jnp.where(leads, lane, twin_ref[pl.ds(at, 1), :] - partner * tile)
        sign = jnp.where(leads, 1.0, -1.0)
        row = lax.broadcasted_iota(jnp.int32, (tile, tile), 0)
        turn[t] = jnp.where(row == spot, sign, 0.0).astype(jnp.bfloat16)
        span = pl.ds(pl.multiple_of(t * tile, tile), tile)
        for u in range(depth // tile):
            keep = jnp.where(rows_ref[t] == cols_ref[u], 1.0, 0.0)
            lanes = slice(u * tile, (u + 1) * tile)
            v_in[span, lanes] = (v_in[span, lanes].astype(jnp.float32) * keep).astype(jnp.bfloat16)
        turned[:, span] = jnp.dot(
            turn[t], v_in[span, :], preferred_element_type=jnp.float32
        ).T.astype(jnp.bfloat16)
        return 0

    lax.fori_loop(0, tiles, prepare, 0)

    def rank_all():
        partners = [mirror_ref[u * tile] // tile for u in range(all_tiles)]

        def one(at, _):
            first = jnp.minimum(at, mirror_ref[at * tile] // tile)
            rank = jnp.int32(0)
            for u in range(all_tiles):
                rank = rank + jnp.where(jnp.logical_and(u < partners[u], u < first), 1, 0)
            rank_ref[at] = rank
            return 0

        lax.fori_loop(0, all_tiles, one, 0)

    load_t.wait()

    def core_copy(q, c):
        return remote(
            prod.at[q, 1 - core, c], from_core.at[q, c],
            core_send.at[q, c], core_recv.at[q, c], intg=sibling,
        )

    def a_copy(q, c):
        return remote(prod.at[q, core, c, :, low], hop_one.at[q, c, :, low],
                      a_send.at[q, c], a_recv.at[q, c], intg=x_peer)

    def b_copy(q, c):
        return remote(prod.at[q, core, c, :, high], hop_one.at[q, c, :, high],
                      b_send.at[q, c], b_recv.at[q, c], intg=y_peer)

    def a2_copy(q, c):
        return remote(prod.at[q, core, c, :, low], hop_two.at[c, :, low],
                      a2_send.at[c], a2_recv.at[c], intg=y_peer)

    def b2_copy(q, c):
        return remote(prod.at[q, core, c, :, high], hop_two.at[c, :, high],
                      b2_send.at[c], b2_recv.at[c], intg=x_peer)

    events = planes * parts

    def multiply(n):
        c, at = n // planes, n % planes
        q = order(at)

        @pl.when(at > 0)
        def _():
            t_copy(t_ref.at[:, c], q, c, t_right, p).wait_recv()

            @pl.when(jnp.logical_and(q < p, p < last))
            def _():
                t_copy(tall.at[q, :, c], q, c, t_right, p + 1).start()

            @pl.when(jnp.logical_and(q > p, p > 0))
            def _():
                t_copy(tall.at[q, :, c], q, c, t_left, p - 1).start()

        @pl.when(jnp.logical_and(at == 1, c + AHEAD < parts))
        def _():
            own_t(c + AHEAD)

        left = tall[q, :, c].reshape(CORES * rows, depth)
        wide = min(256, columns)

        def block(i, _):
            span = pl.ds(pl.multiple_of(i * wide, wide), wide)
            prod[q, :, c, :, span] = jnp.dot(
                left, turned[:, span], preferred_element_type=jnp.float32
            ).reshape(CORES, rows, wide)
            return 0

        lax.fori_loop(0, columns // wide, block, 0)
        core_copy(q, c).start()

    def add_cores(n):
        c, q = n // planes, order(n % planes)
        core_copy(q, c).wait_recv()
        prod[q, core, c] = prod[q, core, c] + from_core[q, c]

        @pl.when(q % 2 != x)
        def _():
            a_copy(q, c).start()

        @pl.when(q // 2 != y)
        def _():
            b_copy(q, c).start()

    def add_first(n):
        c, q = n // planes, order(n % planes)

        @pl.when(q % 2 == x)
        def _():
            a_copy(q, c).wait_recv()
            prod[q, core, c, :, low] = prod[q, core, c, :, low] + hop_one[q, c, :, low]

            @pl.when(q // 2 != y)
            def _():
                a2_copy(q, c).start()

        @pl.when(q // 2 == y)
        def _():
            b_copy(q, c).wait_recv()
            prod[q, core, c, :, high] = prod[q, core, c, :, high] + hop_one[q, c, :, high]

            @pl.when(q % 2 != x)
            def _():
                b2_copy(q, c).start()

    def right_sum(q, c):
        return remote(cont.at[q, c], from_left.at[q, c], zr_send.at[q, c], zr_recv.at[q, c], pair=p + 1)

    def left_sum(q, c):
        return remote(cont.at[q, c], from_right.at[q, c], zl_send.at[q, c], zl_recv.at[q, c], pair=p - 1)

    def pick(k, t):
        return jnp.where(rank_ref[t] == k, 1.0, 0.0)

    def collect(c):
        a2_copy(chip, c).wait_recv()
        b2_copy(chip, c).wait_recv()
        prod[chip, core, c] = prod[chip, core, c] + hop_two[c]

        def fill(k, _):
            total = jnp.zeros((rows, tile), jnp.float32)
            for t in range(tiles):
                total = total + pick(k, base + t) * prod[chip, core, c, :, t * tile : (t + 1) * tile]
            span = pl.ds(pl.multiple_of(k % per_owner * tile, tile), tile)
            cont[k // per_owner, c, :, span] = total
            return 0

        lax.fori_loop(0, OWNERS * per_owner, fill, 0)

        @pl.when(p == 0)
        def _():
            right_sum(1, c).start()
            right_sum(0, c).start()

        @pl.when(p == last)
        def _():
            left_sum(0, c).start()
            left_sum(1, c).start()

    def send_on(c):
        @pl.when(p == 1)
        def _():
            right_sum(1, c).wait_recv()
            cont[1, c] = cont[1, c] + from_left[1, c]
            right_sum(1, c).start()

        @pl.when(p == 2)
        def _():
            left_sum(0, c).wait_recv()
            cont[0, c] = cont[0, c] + from_right[0, c]
            left_sum(0, c).start()

    inner = jnp.logical_and(p > 0, p < last)
    own = jnp.clip(p - 1, 0, OWNERS - 1)

    peer = last - p
    end = jnp.where(p == 1, 0, last)

    def peer_copy(i, c):
        return remote(packs.at[i, c], landed.at[i, c], pack_send.at[i, c], land_recv.at[i, c], pair=peer)

    def end_copy(c):
        return remote(packs.at[2, c], landed.at[0, c], pack_send.at[2, c], land_recv.at[0, c], pair=end)

    def settle(c):
        @pl.when(inner)
        def _():
            right_sum(own, c).wait_recv()
            left_sum(own, c).wait_recv()
            slots[c] = (cont[own, c] + from_left[own, c] + from_right[own, c]).astype(jnp.bfloat16)

            def pack(t, _):
                span = pl.ds(pl.multiple_of(t * tile, tile), tile)
                for i, plane in enumerate((peer, last - end, end, p)):
                    total = jnp.zeros((rows, tile), jnp.float32)
                    for s in range(per_owner):
                        scale = pick(own * per_owner + s, plane * tiles + t)
                        total = total + scale * slots[c, :, s * tile : (s + 1) * tile].astype(jnp.float32)
                    packs[i, c, :, span] = total.astype(jnp.bfloat16)
                return 0

            lax.fori_loop(0, tiles, pack, 0)
            peer_copy(1, c).start()
            peer_copy(0, c).start()

    def merge(c):
        @pl.when(inner)
        def _():
            peer_copy(1, c).wait_recv()
            packs[2, c] = packs[2, c] + landed[1, c]
            end_copy(c).start()

    def emit(c):
        end_copy(c).wait_recv()

        @pl.when(inner)
        def _():
            landed[0, c] = landed[0, c] + packs[3, c]

        def one(t, _):
            span = pl.ds(pl.multiple_of(t * tile, tile), tile)
            out_ref[pl.ds(pl.multiple_of(c * rows, rows), rows), span] = jnp.dot(
                landed[0, c, :, span], turn[t], preferred_element_type=jnp.float32
            ).astype(jnp.bfloat16)
            return 0

        lax.fori_loop(0, tiles, one, 0)

    stages = [collect, send_on, settle, merge, emit]

    def event(n, _):
        @pl.when(n < events)
        def _():
            multiply(n)

        @pl.when(n == 1)
        def _():
            rank_all()

        @pl.when(jnp.logical_and(n >= 1, n < events + 1))
        def _():
            add_cores(n - 1)

        @pl.when(jnp.logical_and(n >= 1 + SPACE, n < events + 1 + SPACE))
        def _():
            add_first(n - 1 - SPACE)

        for at, stage in enumerate(stages):
            since = n - planes - LAG - at * SPACE
            final = since == events - planes - LAG + SPACE
            c = jnp.where(final, parts - 1, jnp.maximum(since, 0) // planes)
            early = jnp.logical_and(jnp.logical_and(since >= 0, since % planes == 0), c < parts - 1)

            @pl.when(jnp.logical_or(final, early))
            def _():
                stage(c)

        return 0

    lax.fori_loop(0, events + 1 + SPACE * len(stages), event, 0)

    def drain(n, _):
        c, q = n // planes, n % planes
        core_copy(q, c).wait_send()

        @pl.when(q % 2 != x)
        def _():
            a_copy(q, c).wait_send()

        @pl.when(q // 2 != y)
        def _():
            b_copy(q, c).wait_send()

        @pl.when(jnp.logical_and(q % 2 == x, q // 2 != y))
        def _():
            a2_copy(q, c).wait_send()

        @pl.when(jnp.logical_and(q % 2 != x, q // 2 == y))
        def _():
            b2_copy(q, c).wait_send()

        @pl.when(jnp.logical_and(q <= p, p < last))
        def _():
            t_copy(tall.at[q, :, c], q, c, t_right, p + 1).wait_send()

        @pl.when(jnp.logical_and(q >= p, p > 0))
        def _():
            t_copy(tall.at[q, :, c], q, c, t_left, p - 1).wait_send()

        @pl.when(jnp.logical_and(q < OWNERS, p == 0))
        def _():
            right_sum(q, c).wait_send()

        @pl.when(jnp.logical_and(q < OWNERS, p == last))
        def _():
            left_sum(q, c).wait_send()

        @pl.when(jnp.logical_and(q == 1, p == 1))
        def _():
            right_sum(q, c).wait_send()

        @pl.when(jnp.logical_and(q == 0, p == 2))
        def _():
            left_sum(q, c).wait_send()

        @pl.when(jnp.logical_and(inner, q < 2))
        def _():
            peer_copy(q, c).wait_send()

        @pl.when(jnp.logical_and(inner, q == 2))
        def _():
            end_copy(c).wait_send()

        return 0

    lax.fori_loop(0, events, drain, 0)


def shards(planes, amplitudes, integrals, sym_rows, sym_cols, mirror_rows):
    tiles = sym_rows.shape[0]
    columns, depth = integrals.shape
    tile = columns // tiles
    all_tiles = mirror_rows.shape[0] // tile
    per_owner = all_tiles // 2 // OWNERS
    rows = amplitudes.shape[0] // (CORES * PARTS)

    dma = pltpu.SemaphoreType.DMA
    grid = (planes, PARTS)
    vmem = pl.BlockSpec(memory_space=pltpu.VMEM)
    smem = pl.BlockSpec(memory_space=pltpu.SMEM)
    hbm = pl.BlockSpec(memory_space=pl.ANY)
    group = per_owner * tile
    return pl.pallas_call(
        functools.partial(ladder_kernel, planes, tiles, tile),
        out_shape=jax.ShapeDtypeStruct((PARTS * rows, columns), jnp.bfloat16),
        in_specs=[hbm, hbm, smem, smem, smem, vmem],
        out_specs=vmem,
        scratch_shapes=[
            pltpu.SMEM((all_tiles,), jnp.int32),
            pltpu.VMEM((tiles, tile, tile), jnp.bfloat16),
            pltpu.VMEM((columns, depth), jnp.bfloat16),
            pltpu.VMEM((depth, columns), jnp.bfloat16),
            pltpu.VMEM((planes, CORES, PARTS, rows, depth), jnp.bfloat16),
            pltpu.VMEM((planes, CORES, PARTS, rows, columns), jnp.float32),
            pltpu.VMEM((planes, PARTS, rows, columns), jnp.float32),
            pltpu.VMEM((planes, PARTS, rows, columns), jnp.float32),
            pltpu.VMEM((PARTS, rows, columns), jnp.float32),
            pltpu.VMEM((OWNERS, PARTS, rows, group), jnp.float32),
            pltpu.VMEM((OWNERS, PARTS, rows, group), jnp.float32),
            pltpu.VMEM((OWNERS, PARTS, rows, group), jnp.float32),
            pltpu.VMEM((PARTS, rows, group), jnp.bfloat16),
            pltpu.VMEM((4, PARTS, rows, columns), jnp.bfloat16),
            pltpu.VMEM((2, PARTS, rows, columns), jnp.bfloat16),
            dma, dma,
            dma(grid), dma(grid), dma(grid), dma(grid), dma(grid),
            dma(grid), dma(grid), dma(grid), dma(grid),
            dma((PARTS,)), dma((PARTS,)), dma((PARTS,)), dma((PARTS,)),
            dma(grid), dma(grid), dma(grid), dma(grid),
            dma((3, PARTS)), dma((2, PARTS)),
        ],
        compiler_params=pltpu.CompilerParams(
            collective_id=0, has_side_effects=True, vmem_limit_bytes=60 * 1024 * 1024
        ),
        cost_estimate=pl.CostEstimate(
            flops=2 * planes * amplitudes.shape[0] * columns * depth,
            bytes_accessed=2 * (amplitudes.size + integrals.size), transcendentals=0,
        ),
    )(amplitudes.reshape(CORES, PARTS, rows, depth), integrals, sym_rows, sym_cols,
      mirror_rows, mirror_rows.reshape(all_tiles, tile))


def solution(mesh):
    planes, chips = mesh.shape["pair"], mesh.shape["intg"] // CORES
    direct = planes == chips and chips == SIDE * SIDE
    body = functools.partial(shards, planes) if direct else shards_plain
    return jax.shard_map(
        body,
        mesh=mesh,
        in_specs=(P("pair", "intg"), P("pair", "intg"), P("pair"), P("intg"), P()),
        out_specs=P("intg", "pair"),
        check_vma=False,
    )
```

```python
import functools

import jax
import jax.numpy as jnp
from jax import lax
from jax.experimental import pallas as pl
from jax.experimental.pallas import tpu as pltpu
from jax.sharding import PartitionSpec as P

MESH = pl.DeviceIdType.MESH
PARTS = 6
LAG = 4
HOP = 2
SPACE = 3
OWNERS = 2
AHEAD = 3
CORES = 2
SIDE = 2


def contract_pair(left, right):
    return lax.dot_general(
        left, right, (((1,), (1,)), ((), ())), preferred_element_type=jnp.float32
    )


def shards_plain(amplitudes, integrals, sym_rows, sym_cols, mirror_rows):
    tile_rows = integrals.shape[0] // sym_rows.shape[0]
    row_sym = jnp.repeat(sym_rows, tile_rows)
    col_sym = jnp.repeat(sym_cols, tile_rows)
    masked = jnp.where(row_sym[:, None] == col_sym[None, :], integrals, jnp.zeros((), jnp.bfloat16))
    ab_rows = integrals.shape[0]
    own_twins = lax.dynamic_slice_in_dim(mirror_rows, lax.axis_index("pair") * ab_rows, ab_rows, 0)
    partial_sums = contract_pair(lax.all_gather(amplitudes, "pair", axis=0, tiled=True), masked)
    result_block = lax.psum_scatter(partial_sums, "intg", scatter_dimension=0, tiled=True)
    all_columns = lax.all_gather(result_block, "pair", axis=1, tiled=True)
    result_block = result_block - jnp.take(all_columns, own_twins, axis=1)
    return result_block.astype(jnp.bfloat16)


def ladder_kernel(
    planes, tiles, tile,
    t_ref, v_ref, rows_ref, cols_ref, mirror_ref, twin_ref, out_ref,
    rank_ref, turn, v_in, turned, tall, prod, from_core, hop_one, hop_two, cont, from_left, from_right, slots,
    v_sem, own_sem, t_recv, t_right, t_left, core_send, core_recv,
    a_send, a_recv, b_send, b_recv, a2_send, a2_recv, b2_send, b2_recv,
    zr_send, zr_recv, zl_send, zl_recv, g_send, g_recv,
):
    parts, rows, depth = t_ref.shape[1], t_ref.shape[2], t_ref.shape[3]
    columns = prod.shape[-1]
    half = columns // 2
    group = cont.shape[-1]
    per_owner = group // tile
    last = planes - 1
    p = lax.axis_index("pair")
    g = lax.axis_index("intg")
    core, x, y = g % 2, (g // 2) % 2, g // 4
    chip = g // 2
    sibling = g + 1 - 2 * core
    x_peer = g + 2 - 4 * x
    y_peer = g + 4 - 8 * y
    low, high = slice(0, half), slice(half, columns)

    def order(step):
        result = jnp.int32(0)
        for plane in range(planes):
            near = sorted(range(planes), key=lambda q: abs(q - plane))
            for at, q in enumerate(near):
                result = result + jnp.where(jnp.logical_and(p == plane, step == at), q, 0)
        return result

    load_v = pltpu.make_async_copy(v_ref, v_in, v_sem)
    load_v.start()
    load_t = pltpu.make_async_copy(t_ref, tall.at[p], own_sem)
    load_t.start()

    barrier = pltpu.get_barrier_semaphore()
    for peer in (sibling, x_peer, y_peer):
        pl.semaphore_signal(barrier, inc=1, device_id={"intg": peer}, device_id_type=MESH)

    for away in range(1, planes):
        pl.semaphore_signal(
            barrier, inc=1, device_id={"pair": (p + away) % planes}, device_id_type=MESH)
    pl.semaphore_wait(barrier, 3 + last)

    def remote(src, dst, send, recv, **where):
        return pltpu.make_async_remote_copy(
            src_ref=src, dst_ref=dst, send_sem=send, recv_sem=recv,
            device_id=where, device_id_type=MESH,
        )

    def t_copy(src, q, c, send, plane):
        return remote(src, tall.at[q, :, c], send.at[q, c], t_recv.at[q, c], pair=plane)

    def own_t(c):
        @pl.when(p < last)
        def _():
            t_copy(t_ref.at[:, c], p, c, t_right, p + 1).start()

        @pl.when(p > 0)
        def _():
            t_copy(t_ref.at[:, c], p, c, t_left, p - 1).start()

    for c in range(AHEAD):
        own_t(c)

    all_tiles = planes * tiles
    base = p * tiles
    partners = [mirror_ref[u * tile] // tile for u in range(all_tiles)]
    load_v.wait()

    def prepare(t, _):
        at = base + t
        partner = mirror_ref[at * tile] // tile
        leads = at < partner
        first = jnp.minimum(at, partner)
        rank = jnp.int32(0)
        for u in range(all_tiles):
            rank = rank + jnp.where(jnp.logical_and(u < partners[u], u < first), 1, 0)
        rank_ref[t] = rank
        lane = lax.broadcasted_iota(jnp.int32, (1, tile), 1)
        spot = jnp.where(leads, lane, twin_ref[pl.ds(at, 1), :] - partner * tile)
        sign = jnp.where(leads, 1.0, -1.0)
        row = lax.broadcasted_iota(jnp.int32, (tile, tile), 0)
        turn[t] = jnp.where(row == spot, sign, 0.0).astype(jnp.bfloat16)
        span = pl.ds(pl.multiple_of(t * tile, tile), tile)
        for u in range(depth // tile):
            keep = jnp.where(rows_ref[t] == cols_ref[u], 1.0, 0.0)
            lanes = slice(u * tile, (u + 1) * tile)
            v_in[span, lanes] = (v_in[span, lanes].astype(jnp.float32) * keep).astype(jnp.bfloat16)
        turned[:, span] = jnp.dot(
            turn[t], v_in[span, :], preferred_element_type=jnp.float32
        ).T.astype(jnp.bfloat16)
        return 0

    lax.fori_loop(0, tiles, prepare, 0)
    load_t.wait()

    def core_copy(q, c):
        return remote(
            prod.at[q, 1 - core, c], from_core.at[q, c],
            core_send.at[q, c], core_recv.at[q, c], intg=sibling,
        )

    def a_copy(q, c):
        return remote(prod.at[q, core, c, :, low], hop_one.at[q, c, :, low],
                      a_send.at[q, c], a_recv.at[q, c], intg=x_peer)

    def b_copy(q, c):
        return remote(prod.at[q, core, c, :, high], hop_one.at[q, c, :, high],
                      b_send.at[q, c], b_recv.at[q, c], intg=y_peer)

    def a2_copy(q, c):
        return remote(prod.at[q, core, c, :, low], hop_two.at[c, :, low],
                      a2_send.at[c], a2_recv.at[c], intg=y_peer)

    def b2_copy(q, c):
        return remote(prod.at[q, core, c, :, high], hop_two.at[c, :, high],
                      b2_send.at[c], b2_recv.at[c], intg=x_peer)

    events = planes * parts

    def multiply(n):
        c, at = n // planes, n % planes
        q = order(at)

        @pl.when(at > 0)
        def _():
            t_copy(t_ref.at[:, c], q, c, t_right, p).wait_recv()

            @pl.when(jnp.logical_and(q < p, p < last))
            def _():
                t_copy(tall.at[q, :, c], q, c, t_right, p + 1).start()

            @pl.when(jnp.logical_and(q > p, p > 0))
            def _():
                t_copy(tall.at[q, :, c], q, c, t_left, p - 1).start()

        @pl.when(jnp.logical_and(at == 1, c + AHEAD < parts))
        def _():
            own_t(c + AHEAD)

        left = tall[q, :, c].reshape(CORES * rows, depth)
        wide = min(256, columns)

        def block(i, _):
            span = pl.ds(pl.multiple_of(i * wide, wide), wide)
            prod[q, :, c, :, span] = jnp.dot(
                left, turned[:, span], preferred_element_type=jnp.float32
            ).reshape(CORES, rows, wide)
            return 0

        lax.fori_loop(0, columns // wide, block, 0)
        core_copy(q, c).start()

    def add_cores(n):
        c, q = n // planes, order(n % planes)
        core_copy(q, c).wait_recv()
        prod[q, core, c] = prod[q, core, c] + from_core[q, c]

        @pl.when(q % 2 != x)
        def _():
            a_copy(q, c).start()

        @pl.when(q // 2 != y)
        def _():
            b_copy(q, c).start()

    def add_first(n):
        c, q = n // planes, order(n % planes)

        @pl.when(q % 2 == x)
        def _():
            a_copy(q, c).wait_recv()
            prod[q, core, c, :, low] = prod[q, core, c, :, low] + hop_one[q, c, :, low]

            @pl.when(q // 2 != y)
            def _():
                a2_copy(q, c).start()

        @pl.when(q // 2 == y)
        def _():
            b_copy(q, c).wait_recv()
            prod[q, core, c, :, high] = prod[q, core, c, :, high] + hop_one[q, c, :, high]

            @pl.when(q % 2 != x)
            def _():
                b2_copy(q, c).start()

    def right_sum(q, c):
        return remote(cont.at[q, c], from_left.at[q, c], zr_send.at[q, c], zr_recv.at[q, c], pair=p + 1)

    def left_sum(q, c):
        return remote(cont.at[q, c], from_right.at[q, c], zl_send.at[q, c], zl_recv.at[q, c], pair=p - 1)

    def pick(k, t):
        return jnp.where(rank_ref[t] == k, 1.0, 0.0)

    def collect(c):
        a2_copy(chip, c).wait_recv()
        b2_copy(chip, c).wait_recv()
        prod[chip, core, c] = prod[chip, core, c] + hop_two[c]

        def fill(k, _):
            total = jnp.zeros((rows, tile), jnp.float32)
            for t in range(tiles):
                total = total + pick(k, t) * prod[chip, core, c, :, t * tile : (t + 1) * tile]
            span = pl.ds(pl.multiple_of(k % per_owner * tile, tile), tile)
            cont[k // per_owner, c, :, span] = total
            return 0

        lax.fori_loop(0, OWNERS * per_owner, fill, 0)

        @pl.when(p == 0)
        def _():
            right_sum(1, c).start()
            right_sum(0, c).start()

        @pl.when(p == last)
        def _():
            left_sum(0, c).start()
            left_sum(1, c).start()

    def send_on(c):
        @pl.when(p == 1)
        def _():
            right_sum(1, c).wait_recv()
            cont[1, c] = cont[1, c] + from_left[1, c]
            right_sum(1, c).start()

        @pl.when(p == 2)
        def _():
            left_sum(0, c).wait_recv()
            cont[0, c] = cont[0, c] + from_right[0, c]
            left_sum(0, c).start()

    def slot_copy(q, c, away, plane):
        return remote(slots.at[q, c], slots.at[q, c], g_send.at[away, c], g_recv.at[q, c], pair=plane)

    inner = jnp.logical_and(p > 0, p < last)
    own = jnp.clip(p - 1, 0, OWNERS - 1)

    def settle(c):
        @pl.when(inner)
        def _():
            right_sum(own, c).wait_recv()
            left_sum(own, c).wait_recv()
            slots[own, c] = (cont[own, c] + from_left[own, c] + from_right[own, c]).astype(jnp.bfloat16)
            for away in range(1, planes):
                slot_copy(own, c, away, (p + away) % planes).start()

    def emit(c):
        for q in range(OWNERS):
            @pl.when(p != q + 1)
            def _():
                slot_copy(q, c, 0, p).wait_recv()

        def one(t, _):
            total = jnp.zeros((rows, tile), jnp.float32)
            for q in range(OWNERS):
                for s in range(per_owner):
                    scale = pick(q * per_owner + s, t)
                    total = total + scale * slots[q, c, :, s * tile : (s + 1) * tile].astype(jnp.float32)
            span = pl.ds(pl.multiple_of(t * tile, tile), tile)
            out_ref[pl.ds(pl.multiple_of(c * rows, rows), rows), span] = jnp.dot(
                total.astype(jnp.bfloat16), turn[t], preferred_element_type=jnp.float32
            ).astype(jnp.bfloat16)
            return 0

        lax.fori_loop(0, tiles, one, 0)

    stages = [collect, send_on, settle, emit]

    def event(n, _):
        @pl.when(n < events)
        def _():
            multiply(n)

        @pl.when(jnp.logical_and(n >= 1, n < events + 1))
        def _():
            add_cores(n - 1)

        @pl.when(jnp.logical_and(n >= 1 + HOP, n < events + 1 + HOP))
        def _():
            add_first(n - 1 - HOP)

        for at, stage in enumerate(stages):
            since = n - planes - LAG - at * SPACE
            final = since == events - planes - LAG + SPACE
            c = jnp.where(final, parts - 1, jnp.maximum(since, 0) // planes)
            early = jnp.logical_and(jnp.logical_and(since >= 0, since % planes == 0), c < parts - 1)

            @pl.when(jnp.logical_or(final, early))
            def _():
                stage(c)

        return 0

    lax.fori_loop(0, events + 1 + SPACE * len(stages), event, 0)

    def drain(n, _):
        c, q = n // planes, n % planes
        core_copy(q, c).wait_send()

        @pl.when(q % 2 != x)
        def _():
            a_copy(q, c).wait_send()

        @pl.when(q // 2 != y)
        def _():
            b_copy(q, c).wait_send()

        @pl.when(jnp.logical_and(q % 2 == x, q // 2 != y))
        def _():
            a2_copy(q, c).wait_send()

        @pl.when(jnp.logical_and(q % 2 != x, q // 2 == y))
        def _():
            b2_copy(q, c).wait_send()

        @pl.when(jnp.logical_and(q <= p, p < last))
        def _():
            t_copy(tall.at[q, :, c], q, c, t_right, p + 1).wait_send()

        @pl.when(jnp.logical_and(q >= p, p > 0))
        def _():
            t_copy(tall.at[q, :, c], q, c, t_left, p - 1).wait_send()

        @pl.when(jnp.logical_and(q < OWNERS, p == 0))
        def _():
            right_sum(q, c).wait_send()

        @pl.when(jnp.logical_and(q < OWNERS, p == last))
        def _():
            left_sum(q, c).wait_send()

        @pl.when(jnp.logical_and(q == 1, p == 1))
        def _():
            right_sum(q, c).wait_send()

        @pl.when(jnp.logical_and(q == 0, p == 2))
        def _():
            left_sum(q, c).wait_send()

        @pl.when(jnp.logical_and(inner, q > 0))
        def _():
            slot_copy(own, c, q, p).wait_send()

        return 0

    lax.fori_loop(0, events, drain, 0)


def shards(planes, amplitudes, integrals, sym_rows, sym_cols, mirror_rows):
    tiles = sym_rows.shape[0]
    columns, depth = integrals.shape
    tile = columns // tiles
    all_tiles = mirror_rows.shape[0] // tile
    per_owner = all_tiles // 2 // OWNERS
    rows = amplitudes.shape[0] // (CORES * PARTS)

    dma = pltpu.SemaphoreType.DMA
    grid = (planes, PARTS)
    vmem = pl.BlockSpec(memory_space=pltpu.VMEM)
    smem = pl.BlockSpec(memory_space=pltpu.SMEM)
    hbm = pl.BlockSpec(memory_space=pl.ANY)
    group = per_owner * tile
    return pl.pallas_call(
        functools.partial(ladder_kernel, planes, tiles, tile),
        out_shape=jax.ShapeDtypeStruct((PARTS * rows, columns), jnp.bfloat16),
        in_specs=[hbm, hbm, smem, smem, smem, vmem],
        out_specs=vmem,
        scratch_shapes=[
            pltpu.SMEM((tiles,), jnp.int32),
            pltpu.VMEM((tiles, tile, tile), jnp.bfloat16),
            pltpu.VMEM((columns, depth), jnp.bfloat16),
            pltpu.VMEM((depth, columns), jnp.bfloat16),
            pltpu.VMEM((planes, CORES, PARTS, rows, depth), jnp.bfloat16),
            pltpu.VMEM((planes, CORES, PARTS, rows, columns), jnp.float32),
            pltpu.VMEM((planes, PARTS, rows, columns), jnp.float32),
            pltpu.VMEM((planes, PARTS, rows, columns), jnp.float32),
            pltpu.VMEM((PARTS, rows, columns), jnp.float32),
            pltpu.VMEM((OWNERS, PARTS, rows, group), jnp.float32),
            pltpu.VMEM((OWNERS, PARTS, rows, group), jnp.float32),
            pltpu.VMEM((OWNERS, PARTS, rows, group), jnp.float32),
            pltpu.VMEM((OWNERS, PARTS, rows, group), jnp.bfloat16),
            dma, dma,
            dma(grid), dma(grid), dma(grid), dma(grid), dma(grid),
            dma(grid), dma(grid), dma(grid), dma(grid),
            dma((PARTS,)), dma((PARTS,)), dma((PARTS,)), dma((PARTS,)),
            dma(grid), dma(grid), dma(grid), dma(grid),
            dma(grid), dma(grid),
        ],
        compiler_params=pltpu.CompilerParams(
            collective_id=0, has_side_effects=True, vmem_limit_bytes=60 * 1024 * 1024
        ),
        cost_estimate=pl.CostEstimate(
            flops=2 * planes * amplitudes.shape[0] * columns * depth,
            bytes_accessed=2 * (amplitudes.size + integrals.size), transcendentals=0,
        ),
    )(amplitudes.reshape(CORES, PARTS, rows, depth), integrals, sym_rows, sym_cols,
      mirror_rows, mirror_rows.reshape(all_tiles, tile))


def solution(mesh):
    planes, chips = mesh.shape["pair"], mesh.shape["intg"] // CORES
    direct = planes == chips and chips == SIDE * SIDE
    body = functools.partial(shards, planes) if direct else shards_plain
    return jax.shard_map(
        body,
        mesh=mesh,
        in_specs=(P("pair", "intg"), P("pair", "intg"), P("pair"), P("intg"), P()),
        out_specs=P("intg", "pair"),
        check_vma=False,
    )
```

```python
import functools

import jax
import jax.numpy as jnp
from jax import lax
from jax.experimental import pallas as pl
from jax.experimental.pallas import tpu as pltpu
from jax.sharding import PartitionSpec as P

MESH = pl.DeviceIdType.MESH
PARTS = 6
LAG = 4
HOP = 2
SPACE = 3
OWNERS = 2
AHEAD = 3
CORES = 2
SIDE = 2


def contract_pair(left, right):
    return lax.dot_general(
        left, right, (((1,), (1,)), ((), ())), preferred_element_type=jnp.float32
    )


def shards_plain(amplitudes, integrals, sym_rows, sym_cols, mirror_rows):
    tile_rows = integrals.shape[0] // sym_rows.shape[0]
    row_sym = jnp.repeat(sym_rows, tile_rows)
    col_sym = jnp.repeat(sym_cols, tile_rows)
    masked = jnp.where(row_sym[:, None] == col_sym[None, :], integrals, jnp.zeros((), jnp.bfloat16))
    ab_rows = integrals.shape[0]
    own_twins = lax.dynamic_slice_in_dim(mirror_rows, lax.axis_index("pair") * ab_rows, ab_rows, 0)
    partial_sums = contract_pair(lax.all_gather(amplitudes, "pair", axis=0, tiled=True), masked)
    result_block = lax.psum_scatter(partial_sums, "intg", scatter_dimension=0, tiled=True)
    all_columns = lax.all_gather(result_block, "pair", axis=1, tiled=True)
    result_block = result_block - jnp.take(all_columns, own_twins, axis=1)
    return result_block.astype(jnp.bfloat16)


def ladder_kernel(
    planes, tiles, tile,
    t_ref, v_ref, rows_ref, cols_ref, mirror_ref, twin_ref, out_ref,
    rank_ref, turn, v_in, turned, tall, prod, from_core, hop_one, hop_two, cont, from_left, from_right, slots,
    v_sem, own_sem, t_recv, t_right, t_left, core_send, core_recv,
    a_send, a_recv, b_send, b_recv, a2_send, a2_recv, b2_send, b2_recv,
    zr_send, zr_recv, zl_send, zl_recv, g_send, g_recv,
):
    parts, rows, depth = t_ref.shape[1], t_ref.shape[2], t_ref.shape[3]
    columns = prod.shape[-1]
    half = columns // 2
    group = cont.shape[-1]
    per_owner = group // tile
    last = planes - 1
    p = lax.axis_index("pair")
    g = lax.axis_index("intg")
    core, x, y = g % 2, (g // 2) % 2, g // 4
    chip = g // 2
    sibling = g + 1 - 2 * core
    x_peer = g + 2 - 4 * x
    y_peer = g + 4 - 8 * y
    low, high = slice(0, half), slice(half, columns)

    def order(step):
        result = jnp.int32(0)
        for plane in range(planes):
            near = sorted(range(planes), key=lambda q: abs(q - plane))
            for at, q in enumerate(near):
                result = result + jnp.where(jnp.logical_and(p == plane, step == at), q, 0)
        return result

    load_v = pltpu.make_async_copy(v_ref, v_in, v_sem)
    load_v.start()
    load_t = pltpu.make_async_copy(t_ref, tall.at[p], own_sem)
    load_t.start()

    barrier = pltpu.get_barrier_semaphore()
    for peer in (sibling, x_peer, y_peer):
        pl.semaphore_signal(barrier, inc=1, device_id={"intg": peer}, device_id_type=MESH)

    for away in range(1, planes):
        pl.semaphore_signal(
            barrier, inc=1, device_id={"pair": (p + away) % planes}, device_id_type=MESH)
    pl.semaphore_wait(barrier, 3 + last)

    def remote(src, dst, send, recv, **where):
        return pltpu.make_async_remote_copy(
            src_ref=src, dst_ref=dst, send_sem=send, recv_sem=recv,
            device_id=where, device_id_type=MESH,
        )

    def t_copy(src, q, c, send, plane):
        return remote(src, tall.at[q, :, c], send.at[q, c], t_recv.at[q, c], pair=plane)

    def own_t(c):
        @pl.when(p < last)
        def _():
            t_copy(t_ref.at[:, c], p, c, t_right, p + 1).start()

        @pl.when(p > 0)
        def _():
            t_copy(t_ref.at[:, c], p, c, t_left, p - 1).start()

    for c in range(AHEAD):
        own_t(c)

    all_tiles = planes * tiles
    base = p * tiles
    partners = [mirror_ref[u * tile] // tile for u in range(all_tiles)]
    load_v.wait()

    def prepare(t, _):
        at = base + t
        partner = mirror_ref[at * tile] // tile
        leads = at < partner
        first = jnp.minimum(at, partner)
        rank = jnp.int32(0)
        for u in range(all_tiles):
            rank = rank + jnp.where(jnp.logical_and(u < partners[u], u < first), 1, 0)
        rank_ref[t] = rank
        lane = lax.broadcasted_iota(jnp.int32, (1, tile), 1)
        spot = jnp.where(leads, lane, twin_ref[pl.ds(at, 1), :] - partner * tile)
        sign = jnp.where(leads, 1.0, -1.0)
        row = lax.broadcasted_iota(jnp.int32, (tile, tile), 0)
        turn[t] = jnp.where(row == spot, sign, 0.0).astype(jnp.bfloat16)
        span = pl.ds(pl.multiple_of(t * tile, tile), tile)
        for u in range(depth // tile):
            keep = jnp.where(rows_ref[t] == cols_ref[u], 1.0, 0.0)
            lanes = slice(u * tile, (u + 1) * tile)
            v_in[span, lanes] = (v_in[span, lanes].astype(jnp.float32) * keep).astype(jnp.bfloat16)
        turned[:, span] = jnp.dot(
            turn[t], v_in[span, :], preferred_element_type=jnp.float32
        ).T.astype(jnp.bfloat16)
        return 0

    lax.fori_loop(0, tiles, prepare, 0)
    load_t.wait()

    def core_copy(q, c):
        return remote(
            prod.at[q, 1 - core, c], from_core.at[q, c],
            core_send.at[q, c], core_recv.at[q, c], intg=sibling,
        )

    def a_copy(q, c):
        return remote(prod.at[q, core, c, :, low], hop_one.at[q, c, :, low],
                      a_send.at[q, c], a_recv.at[q, c], intg=x_peer)

    def b_copy(q, c):
        return remote(prod.at[q, core, c, :, high], hop_one.at[q, c, :, high],
                      b_send.at[q, c], b_recv.at[q, c], intg=y_peer)

    def a2_copy(q, c):
        return remote(prod.at[q, core, c, :, low], hop_two.at[c, :, low],
                      a2_send.at[c], a2_recv.at[c], intg=y_peer)

    def b2_copy(q, c):
        return remote(prod.at[q, core, c, :, high], hop_two.at[c, :, high],
                      b2_send.at[c], b2_recv.at[c], intg=x_peer)

    events = planes * parts
    wide = min(256, columns)

    def own_block(i, _):
        span = pl.ds(pl.multiple_of(i * wide, wide), wide)
        prod[p, :, :, :, span] = jnp.dot(
            tall[p].reshape(CORES * parts * rows, depth), turned[:, span],
            preferred_element_type=jnp.float32,
        ).reshape(CORES, parts, rows, wide)
        return 0

    lax.fori_loop(0, columns // wide, own_block, 0)

    def multiply(n):
        c, at = n // planes, n % planes
        q = order(at)

        @pl.when(at > 0)
        def _():
            t_copy(t_ref.at[:, c], q, c, t_right, p).wait_recv()

            @pl.when(jnp.logical_and(q < p, p < last))
            def _():
                t_copy(tall.at[q, :, c], q, c, t_right, p + 1).start()

            @pl.when(jnp.logical_and(q > p, p > 0))
            def _():
                t_copy(tall.at[q, :, c], q, c, t_left, p - 1).start()

        @pl.when(jnp.logical_and(at == 1, c + AHEAD < parts))
        def _():
            own_t(c + AHEAD)

        @pl.when(at > 0)
        def _():
            left = tall[q, :, c].reshape(CORES * rows, depth)

            def block(i, _):
                span = pl.ds(pl.multiple_of(i * wide, wide), wide)
                prod[q, :, c, :, span] = jnp.dot(
                    left, turned[:, span], preferred_element_type=jnp.float32
                ).reshape(CORES, rows, wide)
                return 0

            lax.fori_loop(0, columns // wide, block, 0)

        core_copy(q, c).start()

    def add_cores(n):
        c, q = n // planes, order(n % planes)
        core_copy(q, c).wait_recv()
        prod[q, core, c] = prod[q, core, c] + from_core[q, c]

        @pl.when(q % 2 != x)
        def _():
            a_copy(q, c).start()

        @pl.when(q // 2 != y)
        def _():
            b_copy(q, c).start()

    def add_first(n):
        c, q = n // planes, order(n % planes)

        @pl.when(q % 2 == x)
        def _():
            a_copy(q, c).wait_recv()
            prod[q, core, c, :, low] = prod[q, core, c, :, low] + hop_one[q, c, :, low]

            @pl.when(q // 2 != y)
            def _():
                a2_copy(q, c).start()

        @pl.when(q // 2 == y)
        def _():
            b_copy(q, c).wait_recv()
            prod[q, core, c, :, high] = prod[q, core, c, :, high] + hop_one[q, c, :, high]

            @pl.when(q % 2 != x)
            def _():
                b2_copy(q, c).start()

    def right_sum(q, c):
        return remote(cont.at[q, c], from_left.at[q, c], zr_send.at[q, c], zr_recv.at[q, c], pair=p + 1)

    def left_sum(q, c):
        return remote(cont.at[q, c], from_right.at[q, c], zl_send.at[q, c], zl_recv.at[q, c], pair=p - 1)

    def pick(k, t):
        return jnp.where(rank_ref[t] == k, 1.0, 0.0)

    def collect(c):
        a2_copy(chip, c).wait_recv()
        b2_copy(chip, c).wait_recv()
        prod[chip, core, c] = prod[chip, core, c] + hop_two[c]

        def fill(k, _):
            total = jnp.zeros((rows, tile), jnp.float32)
            for t in range(tiles):
                total = total + pick(k, t) * prod[chip, core, c, :, t * tile : (t + 1) * tile]
            span = pl.ds(pl.multiple_of(k % per_owner * tile, tile), tile)
            cont[k // per_owner, c, :, span] = total
            return 0

        lax.fori_loop(0, OWNERS * per_owner, fill, 0)

        @pl.when(p == 0)
        def _():
            right_sum(1, c).start()
            right_sum(0, c).start()

        @pl.when(p == last)
        def _():
            left_sum(0, c).start()
            left_sum(1, c).start()

    def send_on(c):
        @pl.when(p == 1)
        def _():
            right_sum(1, c).wait_recv()
            cont[1, c] = cont[1, c] + from_left[1, c]
            right_sum(1, c).start()

        @pl.when(p == 2)
        def _():
            left_sum(0, c).wait_recv()
            cont[0, c] = cont[0, c] + from_right[0, c]
            left_sum(0, c).start()

    def slot_copy(q, c, away, plane):
        return remote(slots.at[q, c], slots.at[q, c], g_send.at[away, c], g_recv.at[q, c], pair=plane)

    inner = jnp.logical_and(p > 0, p < last)
    own = jnp.clip(p - 1, 0, OWNERS - 1)

    def settle(c):
        @pl.when(inner)
        def _():
            right_sum(own, c).wait_recv()
            left_sum(own, c).wait_recv()
            slots[own, c] = (cont[own, c] + from_left[own, c] + from_right[own, c]).astype(jnp.bfloat16)
            for away in range(1, planes):
                slot_copy(own, c, away, (p + away) % planes).start()

    def emit(c):
        for q in range(OWNERS):
            @pl.when(p != q + 1)
            def _():
                slot_copy(q, c, 0, p).wait_recv()

        def one(t, _):
            total = jnp.zeros((rows, tile), jnp.float32)
            for q in range(OWNERS):
                for s in range(per_owner):
                    scale = pick(q * per_owner + s, t)
                    total = total + scale * slots[q, c, :, s * tile : (s + 1) * tile].astype(jnp.float32)
            span = pl.ds(pl.multiple_of(t * tile, tile), tile)
            out_ref[pl.ds(pl.multiple_of(c * rows, rows), rows), span] = jnp.dot(
                total.astype(jnp.bfloat16), turn[t], preferred_element_type=jnp.float32
            ).astype(jnp.bfloat16)
            return 0

        lax.fori_loop(0, tiles, one, 0)

    stages = [collect, send_on, settle, emit]

    def event(n, _):
        @pl.when(n < events)
        def _():
            multiply(n)

        @pl.when(jnp.logical_and(n >= 1, n < events + 1))
        def _():
            add_cores(n - 1)

        @pl.when(jnp.logical_and(n >= 1 + HOP, n < events + 1 + HOP))
        def _():
            add_first(n - 1 - HOP)

        for at, stage in enumerate(stages):
            since = n - planes - LAG - at * SPACE
            final = since == events - planes - LAG + SPACE
            c = jnp.where(final, parts - 1, jnp.maximum(since, 0) // planes)
            early = jnp.logical_and(jnp.logical_and(since >= 0, since % planes == 0), c < parts - 1)

            @pl.when(jnp.logical_or(final, early))
            def _():
                stage(c)

        return 0

    lax.fori_loop(0, events + 1 + SPACE * len(stages), event, 0)

    def drain(n, _):
        c, q = n // planes, n % planes
        core_copy(q, c).wait_send()

        @pl.when(q % 2 != x)
        def _():
            a_copy(q, c).wait_send()

        @pl.when(q // 2 != y)
        def _():
            b_copy(q, c).wait_send()

        @pl.when(jnp.logical_and(q % 2 == x, q // 2 != y))
        def _():
            a2_copy(q, c).wait_send()

        @pl.when(jnp.logical_and(q % 2 != x, q // 2 == y))
        def _():
            b2_copy(q, c).wait_send()

        @pl.when(jnp.logical_and(q <= p, p < last))
        def _():
            t_copy(tall.at[q, :, c], q, c, t_right, p + 1).wait_send()

        @pl.when(jnp.logical_and(q >= p, p > 0))
        def _():
            t_copy(tall.at[q, :, c], q, c, t_left, p - 1).wait_send()

        @pl.when(jnp.logical_and(q < OWNERS, p == 0))
        def _():
            right_sum(q, c).wait_send()

        @pl.when(jnp.logical_and(q < OWNERS, p == last))
        def _():
            left_sum(q, c).wait_send()

        @pl.when(jnp.logical_and(q == 1, p == 1))
        def _():
            right_sum(q, c).wait_send()

        @pl.when(jnp.logical_and(q == 0, p == 2))
        def _():
            left_sum(q, c).wait_send()

        @pl.when(jnp.logical_and(inner, q > 0))
        def _():
            slot_copy(own, c, q, p).wait_send()

        return 0

    lax.fori_loop(0, events, drain, 0)


def shards(planes, amplitudes, integrals, sym_rows, sym_cols, mirror_rows):
    tiles = sym_rows.shape[0]
    columns, depth = integrals.shape
    tile = columns // tiles
    all_tiles = mirror_rows.shape[0] // tile
    per_owner = all_tiles // 2 // OWNERS
    rows = amplitudes.shape[0] // (CORES * PARTS)

    dma = pltpu.SemaphoreType.DMA
    grid = (planes, PARTS)
    vmem = pl.BlockSpec(memory_space=pltpu.VMEM)
    smem = pl.BlockSpec(memory_space=pltpu.SMEM)
    hbm = pl.BlockSpec(memory_space=pl.ANY)
    group = per_owner * tile
    return pl.pallas_call(
        functools.partial(ladder_kernel, planes, tiles, tile),
        out_shape=jax.ShapeDtypeStruct((PARTS * rows, columns), jnp.bfloat16),
        in_specs=[hbm, hbm, smem, smem, smem, vmem],
        out_specs=vmem,
        scratch_shapes=[
            pltpu.SMEM((tiles,), jnp.int32),
            pltpu.VMEM((tiles, tile, tile), jnp.bfloat16),
            pltpu.VMEM((columns, depth), jnp.bfloat16),
            pltpu.VMEM((depth, columns), jnp.bfloat16),
            pltpu.VMEM((planes, CORES, PARTS, rows, depth), jnp.bfloat16),
            pltpu.VMEM((planes, CORES, PARTS, rows, columns), jnp.float32),
            pltpu.VMEM((planes, PARTS, rows, columns), jnp.float32),
            pltpu.VMEM((planes, PARTS, rows, columns), jnp.float32),
            pltpu.VMEM((PARTS, rows, columns), jnp.float32),
            pltpu.VMEM((OWNERS, PARTS, rows, group), jnp.float32),
            pltpu.VMEM((OWNERS, PARTS, rows, group), jnp.float32),
            pltpu.VMEM((OWNERS, PARTS, rows, group), jnp.float32),
            pltpu.VMEM((OWNERS, PARTS, rows, group), jnp.bfloat16),
            dma, dma,
            dma(grid), dma(grid), dma(grid), dma(grid), dma(grid),
            dma(grid), dma(grid), dma(grid), dma(grid),
            dma((PARTS,)), dma((PARTS,)), dma((PARTS,)), dma((PARTS,)),
            dma(grid), dma(grid), dma(grid), dma(grid),
            dma(grid), dma(grid),
        ],
        compiler_params=pltpu.CompilerParams(
            collective_id=0, has_side_effects=True, vmem_limit_bytes=60 * 1024 * 1024
        ),
        cost_estimate=pl.CostEstimate(
            flops=2 * planes * amplitudes.shape[0] * columns * depth,
            bytes_accessed=2 * (amplitudes.size + integrals.size), transcendentals=0,
        ),
    )(amplitudes.reshape(CORES, PARTS, rows, depth), integrals, sym_rows, sym_cols,
      mirror_rows, mirror_rows.reshape(all_tiles, tile))


def solution(mesh):
    planes, chips = mesh.shape["pair"], mesh.shape["intg"] // CORES
    direct = planes == chips and chips == SIDE * SIDE
    body = functools.partial(shards, planes) if direct else shards_plain
    return jax.shard_map(
        body,
        mesh=mesh,
        in_specs=(P("pair", "intg"), P("pair", "intg"), P("pair"), P("intg"), P()),
        out_specs=P("intg", "pair"),
        check_vma=False,
    )
```

```python
import functools

import jax
import jax.numpy as jnp
from jax import lax
from jax.experimental import pallas as pl
from jax.experimental.pallas import tpu as pltpu
from jax.sharding import PartitionSpec as P

MESH = pl.DeviceIdType.MESH
PARTS = 6
LAG = 3
HOP = 2
SPACE = 3
OWNERS = 2
AHEAD = 3
CORES = 2
SIDE = 2


def contract_pair(left, right):
    return lax.dot_general(
        left, right, (((1,), (1,)), ((), ())), preferred_element_type=jnp.float32
    )


def shards_plain(amplitudes, integrals, sym_rows, sym_cols, mirror_rows):
    tile_rows = integrals.shape[0] // sym_rows.shape[0]
    row_sym = jnp.repeat(sym_rows, tile_rows)
    col_sym = jnp.repeat(sym_cols, tile_rows)
    masked = jnp.where(row_sym[:, None] == col_sym[None, :], integrals, jnp.zeros((), jnp.bfloat16))
    ab_rows = integrals.shape[0]
    own_twins = lax.dynamic_slice_in_dim(mirror_rows, lax.axis_index("pair") * ab_rows, ab_rows, 0)
    partial_sums = contract_pair(lax.all_gather(amplitudes, "pair", axis=0, tiled=True), masked)
    result_block = lax.psum_scatter(partial_sums, "intg", scatter_dimension=0, tiled=True)
    all_columns = lax.all_gather(result_block, "pair", axis=1, tiled=True)
    result_block = result_block - jnp.take(all_columns, own_twins, axis=1)
    return result_block.astype(jnp.bfloat16)


def ladder_kernel(
    planes, tiles, tile,
    t_ref, v_ref, rows_ref, cols_ref, mirror_ref, twin_ref, out_ref,
    rank_ref, turn, v_in, turned, tall, prod, from_core, hop_one, hop_two, cont, from_left, from_right, slots,
    v_sem, own_sem, t_recv, t_right, t_left, core_send, core_recv,
    a_send, a_recv, b_send, b_recv, a2_send, a2_recv, b2_send, b2_recv,
    zr_send, zr_recv, zl_send, zl_recv, g_send, g_recv,
):
    parts, rows, depth = t_ref.shape[1], t_ref.shape[2], t_ref.shape[3]
    columns = prod.shape[-1]
    half = columns // 2
    group = cont.shape[-1]
    per_owner = group // tile
    last = planes - 1
    p = lax.axis_index("pair")
    g = lax.axis_index("intg")
    core, x, y = g % 2, (g // 2) % 2, g // 4
    chip = g // 2
    sibling = g + 1 - 2 * core
    x_peer = g + 2 - 4 * x
    y_peer = g + 4 - 8 * y
    low, high = slice(0, half), slice(half, columns)

    def order(step):
        result = jnp.int32(0)
        for plane in range(planes):
            near = sorted(range(planes), key=lambda q: abs(q - plane))
            for at, q in enumerate(near):
                result = result + jnp.where(jnp.logical_and(p == plane, step == at), q, 0)
        return result

    load_v = pltpu.make_async_copy(v_ref, v_in, v_sem)
    load_v.start()
    load_t = pltpu.make_async_copy(t_ref, tall.at[p], own_sem)
    load_t.start()

    barrier = pltpu.get_barrier_semaphore()
    for peer in (sibling, x_peer, y_peer):
        pl.semaphore_signal(barrier, inc=1, device_id={"intg": peer}, device_id_type=MESH)

    for away in range(1, planes):
        pl.semaphore_signal(
            barrier, inc=1, device_id={"pair": (p + away) % planes}, device_id_type=MESH)
    pl.semaphore_wait(barrier, 3 + last)

    def remote(src, dst, send, recv, **where):
        return pltpu.make_async_remote_copy(
            src_ref=src, dst_ref=dst, send_sem=send, recv_sem=recv,
            device_id=where, device_id_type=MESH,
        )

    def t_copy(src, q, c, send, plane):
        return remote(src, tall.at[q, :, c], send.at[q, c], t_recv.at[q, c], pair=plane)

    def own_t(c):
        @pl.when(p < last)
        def _():
            t_copy(t_ref.at[:, c], p, c, t_right, p + 1).start()

        @pl.when(p > 0)
        def _():
            t_copy(t_ref.at[:, c], p, c, t_left, p - 1).start()

    for c in range(AHEAD):
        own_t(c)

    all_tiles = planes * tiles
    base = p * tiles
    partners = [mirror_ref[u * tile] // tile for u in range(all_tiles)]
    load_v.wait()

    def prepare(t, _):
        at = base + t
        partner = mirror_ref[at * tile] // tile
        leads = at < partner
        first = jnp.minimum(at, partner)
        rank = jnp.int32(0)
        for u in range(all_tiles):
            rank = rank + jnp.where(jnp.logical_and(u < partners[u], u < first), 1, 0)
        rank_ref[t] = rank
        lane = lax.broadcasted_iota(jnp.int32, (1, tile), 1)
        spot = jnp.where(leads, lane, twin_ref[pl.ds(at, 1), :] - partner * tile)
        sign = jnp.where(leads, 1.0, -1.0)
        row = lax.broadcasted_iota(jnp.int32, (tile, tile), 0)
        turn[t] = jnp.where(row == spot, sign, 0.0).astype(jnp.bfloat16)
        span = pl.ds(pl.multiple_of(t * tile, tile), tile)
        for u in range(depth // tile):
            keep = jnp.where(rows_ref[t] == cols_ref[u], 1.0, 0.0)
            lanes = slice(u * tile, (u + 1) * tile)
            v_in[span, lanes] = (v_in[span, lanes].astype(jnp.float32) * keep).astype(jnp.bfloat16)
        turned[:, span] = jnp.dot(
            turn[t], v_in[span, :], preferred_element_type=jnp.float32
        ).T.astype(jnp.bfloat16)
        return 0

    lax.fori_loop(0, tiles, prepare, 0)
    load_t.wait()

    def core_copy(q, c):
        return remote(
            prod.at[q, 1 - core, c], from_core.at[q, c],
            core_send.at[q, c], core_recv.at[q, c], intg=sibling,
        )

    def a_copy(q, c):
        return remote(prod.at[q, core, c, :, low], hop_one.at[q, c, :, low],
                      a_send.at[q, c], a_recv.at[q, c], intg=x_peer)

    def b_copy(q, c):
        return remote(prod.at[q, core, c, :, high], hop_one.at[q, c, :, high],
                      b_send.at[q, c], b_recv.at[q, c], intg=y_peer)

    def a2_copy(q, c):
        return remote(prod.at[q, core, c, :, low], hop_two.at[c, :, low],
                      a2_send.at[c], a2_recv.at[c], intg=y_peer)

    def b2_copy(q, c):
        return remote(prod.at[q, core, c, :, high], hop_two.at[c, :, high],
                      b2_send.at[c], b2_recv.at[c], intg=x_peer)

    events = planes * parts
    wide = min(256, columns)

    def own_block(i, _):
        span = pl.ds(pl.multiple_of(i * wide, wide), wide)
        prod[p, :, :, :, span] = jnp.dot(
            tall[p].reshape(CORES * parts * rows, depth), turned[:, span],
            preferred_element_type=jnp.float32,
        ).reshape(CORES, parts, rows, wide)
        return 0

    lax.fori_loop(0, columns // wide, own_block, 0)

    def multiply(n):
        c, at = n // planes, n % planes
        q = order(at)

        @pl.when(at > 0)
        def _():
            t_copy(t_ref.at[:, c], q, c, t_right, p).wait_recv()

            @pl.when(jnp.logical_and(q < p, p < last))
            def _():
                t_copy(tall.at[q, :, c], q, c, t_right, p + 1).start()

            @pl.when(jnp.logical_and(q > p, p > 0))
            def _():
                t_copy(tall.at[q, :, c], q, c, t_left, p - 1).start()

        @pl.when(jnp.logical_and(at == 1, c + AHEAD < parts))
        def _():
            own_t(c + AHEAD)

        @pl.when(at > 0)
        def _():
            left = tall[q, :, c].reshape(CORES * rows, depth)

            def block(i, _):
                span = pl.ds(pl.multiple_of(i * wide, wide), wide)
                prod[q, :, c, :, span] = jnp.dot(
                    left, turned[:, span], preferred_element_type=jnp.float32
                ).reshape(CORES, rows, wide)
                return 0

            lax.fori_loop(0, columns // wide, block, 0)

        core_copy(q, c).start()

    def add_cores(n):
        c, q = n // planes, order(n % planes)
        core_copy(q, c).wait_recv()
        prod[q, core, c] = prod[q, core, c] + from_core[q, c]

        @pl.when(q % 2 != x)
        def _():
            a_copy(q, c).start()

        @pl.when(q // 2 != y)
        def _():
            b_copy(q, c).start()

    def add_first(n):
        c, q = n // planes, order(n % planes)

        @pl.when(q % 2 == x)
        def _():
            a_copy(q, c).wait_recv()
            prod[q, core, c, :, low] = prod[q, core, c, :, low] + hop_one[q, c, :, low]

            @pl.when(q // 2 != y)
            def _():
                a2_copy(q, c).start()

        @pl.when(q // 2 == y)
        def _():
            b_copy(q, c).wait_recv()
            prod[q, core, c, :, high] = prod[q, core, c, :, high] + hop_one[q, c, :, high]

            @pl.when(q % 2 != x)
            def _():
                b2_copy(q, c).start()

    def right_sum(q, c):
        return remote(cont.at[q, c], from_left.at[q, c], zr_send.at[q, c], zr_recv.at[q, c], pair=p + 1)

    def left_sum(q, c):
        return remote(cont.at[q, c], from_right.at[q, c], zl_send.at[q, c], zl_recv.at[q, c], pair=p - 1)

    def pick(k, t):
        return jnp.where(rank_ref[t] == k, 1.0, 0.0)

    def collect(c):
        a2_copy(chip, c).wait_recv()
        b2_copy(chip, c).wait_recv()
        prod[chip, core, c] = prod[chip, core, c] + hop_two[c]

        def fill(k, _):
            total = jnp.zeros((rows, tile), jnp.float32)
            for t in range(tiles):
                total = total + pick(k, t) * prod[chip, core, c, :, t * tile : (t + 1) * tile]
            span = pl.ds(pl.multiple_of(k % per_owner * tile, tile), tile)
            cont[k // per_owner, c, :, span] = total
            return 0

        lax.fori_loop(0, OWNERS * per_owner, fill, 0)

        @pl.when(p == 0)
        def _():
            right_sum(1, c).start()
            right_sum(0, c).start()

        @pl.when(p == last)
        def _():
            left_sum(0, c).start()
            left_sum(1, c).start()

    def send_on(c):
        @pl.when(p == 1)
        def _():
            right_sum(1, c).wait_recv()
            cont[1, c] = cont[1, c] + from_left[1, c]
            right_sum(1, c).start()

        @pl.when(p == 2)
        def _():
            left_sum(0, c).wait_recv()
            cont[0, c] = cont[0, c] + from_right[0, c]
            left_sum(0, c).start()

    def slot_copy(q, c, away, plane):
        return remote(slots.at[q, c], slots.at[q, c], g_send.at[away, c], g_recv.at[q, c], pair=plane)

    inner = jnp.logical_and(p > 0, p < last)
    own = jnp.clip(p - 1, 0, OWNERS - 1)

    def settle(c):
        @pl.when(inner)
        def _():
            right_sum(own, c).wait_recv()
            left_sum(own, c).wait_recv()
            slots[own, c] = (cont[own, c] + from_left[own, c] + from_right[own, c]).astype(jnp.bfloat16)
            for away in range(1, planes):
                slot_copy(own, c, away, (p + away) % planes).start()

    def emit(c):
        for q in range(OWNERS):
            @pl.when(p != q + 1)
            def _():
                slot_copy(q, c, 0, p).wait_recv()

        def one(t, _):
            total = jnp.zeros((rows, tile), jnp.float32)
            for q in range(OWNERS):
                for s in range(per_owner):
                    scale = pick(q * per_owner + s, t)
                    total = total + scale * slots[q, c, :, s * tile : (s + 1) * tile].astype(jnp.float32)
            span = pl.ds(pl.multiple_of(t * tile, tile), tile)
            out_ref[pl.ds(pl.multiple_of(c * rows, rows), rows), span] = jnp.dot(
                total.astype(jnp.bfloat16), turn[t], preferred_element_type=jnp.float32
            ).astype(jnp.bfloat16)
            return 0

        lax.fori_loop(0, tiles, one, 0)

    stages = [collect, send_on, settle, emit]

    def event(n, _):
        @pl.when(n < events)
        def _():
            multiply(n)

        @pl.when(jnp.logical_and(n >= 1, n < events + 1))
        def _():
            add_cores(n - 1)

        @pl.when(jnp.logical_and(n >= 1 + HOP, n < events + 1 + HOP))
        def _():
            add_first(n - 1 - HOP)

        for at, stage in enumerate(stages):
            since = n - planes - LAG - at * SPACE
            final = since == events - planes - LAG + SPACE
            c = jnp.where(final, parts - 1, jnp.maximum(since, 0) // planes)
            early = jnp.logical_and(jnp.logical_and(since >= 0, since % planes == 0), c < parts - 1)

            @pl.when(jnp.logical_or(final, early))
            def _():
                stage(c)

        return 0

    lax.fori_loop(0, events + 1 + SPACE * len(stages), event, 0)

    def drain(n, _):
        c, q = n // planes, n % planes
        core_copy(q, c).wait_send()

        @pl.when(q % 2 != x)
        def _():
            a_copy(q, c).wait_send()

        @pl.when(q // 2 != y)
        def _():
            b_copy(q, c).wait_send()

        @pl.when(jnp.logical_and(q % 2 == x, q // 2 != y))
        def _():
            a2_copy(q, c).wait_send()

        @pl.when(jnp.logical_and(q % 2 != x, q // 2 == y))
        def _():
            b2_copy(q, c).wait_send()

        @pl.when(jnp.logical_and(q <= p, p < last))
        def _():
            t_copy(tall.at[q, :, c], q, c, t_right, p + 1).wait_send()

        @pl.when(jnp.logical_and(q >= p, p > 0))
        def _():
            t_copy(tall.at[q, :, c], q, c, t_left, p - 1).wait_send()

        @pl.when(jnp.logical_and(q < OWNERS, p == 0))
        def _():
            right_sum(q, c).wait_send()

        @pl.when(jnp.logical_and(q < OWNERS, p == last))
        def _():
            left_sum(q, c).wait_send()

        @pl.when(jnp.logical_and(q == 1, p == 1))
        def _():
            right_sum(q, c).wait_send()

        @pl.when(jnp.logical_and(q == 0, p == 2))
        def _():
            left_sum(q, c).wait_send()

        @pl.when(jnp.logical_and(inner, q > 0))
        def _():
            slot_copy(own, c, q, p).wait_send()

        return 0

    lax.fori_loop(0, events, drain, 0)


def shards(planes, amplitudes, integrals, sym_rows, sym_cols, mirror_rows):
    tiles = sym_rows.shape[0]
    columns, depth = integrals.shape
    tile = columns // tiles
    all_tiles = mirror_rows.shape[0] // tile
    per_owner = all_tiles // 2 // OWNERS
    rows = amplitudes.shape[0] // (CORES * PARTS)

    dma = pltpu.SemaphoreType.DMA
    grid = (planes, PARTS)
    vmem = pl.BlockSpec(memory_space=pltpu.VMEM)
    smem = pl.BlockSpec(memory_space=pltpu.SMEM)
    hbm = pl.BlockSpec(memory_space=pl.ANY)
    group = per_owner * tile
    return pl.pallas_call(
        functools.partial(ladder_kernel, planes, tiles, tile),
        out_shape=jax.ShapeDtypeStruct((PARTS * rows, columns), jnp.bfloat16),
        in_specs=[hbm, hbm, smem, smem, smem, vmem],
        out_specs=vmem,
        scratch_shapes=[
            pltpu.SMEM((tiles,), jnp.int32),
            pltpu.VMEM((tiles, tile, tile), jnp.bfloat16),
            pltpu.VMEM((columns, depth), jnp.bfloat16),
            pltpu.VMEM((depth, columns), jnp.bfloat16),
            pltpu.VMEM((planes, CORES, PARTS, rows, depth), jnp.bfloat16),
            pltpu.VMEM((planes, CORES, PARTS, rows, columns), jnp.float32),
            pltpu.VMEM((planes, PARTS, rows, columns), jnp.float32),
            pltpu.VMEM((planes, PARTS, rows, columns), jnp.float32),
            pltpu.VMEM((PARTS, rows, columns), jnp.float32),
            pltpu.VMEM((OWNERS, PARTS, rows, group), jnp.float32),
            pltpu.VMEM((OWNERS, PARTS, rows, group), jnp.float32),
            pltpu.VMEM((OWNERS, PARTS, rows, group), jnp.float32),
            pltpu.VMEM((OWNERS, PARTS, rows, group), jnp.bfloat16),
            dma, dma,
            dma(grid), dma(grid), dma(grid), dma(grid), dma(grid),
            dma(grid), dma(grid), dma(grid), dma(grid),
            dma((PARTS,)), dma((PARTS,)), dma((PARTS,)), dma((PARTS,)),
            dma(grid), dma(grid), dma(grid), dma(grid),
            dma(grid), dma(grid),
        ],
        compiler_params=pltpu.CompilerParams(
            collective_id=0, has_side_effects=True, vmem_limit_bytes=60 * 1024 * 1024
        ),
        cost_estimate=pl.CostEstimate(
            flops=2 * planes * amplitudes.shape[0] * columns * depth,
            bytes_accessed=2 * (amplitudes.size + integrals.size), transcendentals=0,
        ),
    )(amplitudes.reshape(CORES, PARTS, rows, depth), integrals, sym_rows, sym_cols,
      mirror_rows, mirror_rows.reshape(all_tiles, tile))


def solution(mesh):
    planes, chips = mesh.shape["pair"], mesh.shape["intg"] // CORES
    direct = planes == chips and chips == SIDE * SIDE
    body = functools.partial(shards, planes) if direct else shards_plain
    return jax.shard_map(
        body,
        mesh=mesh,
        in_specs=(P("pair", "intg"), P("pair", "intg"), P("pair"), P("intg"), P()),
        out_specs=P("intg", "pair"),
        check_vma=False,
    )
```
